32 devices in a mesh: groups: 2 (over x), seq: 16 (over z, y, core).
Axes of the slice: x: 2, y: 2, z: 4, core: 2. Of those that a mesh axis runs over, the one named last changes fastest.
Arguments:
- block_mask: int32 [64, 32], P(('groups', 'seq')), parts along dimension 0, may hold values from 0 to 1, as said below
- queries: bfloat16 [8192, 20, 128], P(('groups', 'seq')), parts along dimension 0, may hold values from -64 to 64
- keys: bfloat16 [8192, 4, 128], P(('groups', 'seq')), parts along dimension 0, may hold values from -64 to 64
- values: bfloat16 [8192, 4, 128], P(('groups', 'seq')), parts along dimension 0, may hold values from -6 to 6
- output_gradient: bfloat16 [8192, 20, 128], P(('groups', 'seq')), parts along dimension 0, may hold values from -6 to 6
Outputs:
- attended: bfloat16 [8192, 20, 128], P(('groups', 'seq')), parts along dimension 0
- grad_queries: bfloat16 [8192, 20, 128], P(('groups', 'seq')), parts along dimension 0
- grad_keys: bfloat16 [8192, 4, 128], P(('groups', 'seq')), parts along dimension 0
- grad_values: bfloat16 [8192, 4, 128], P(('groups', 'seq')), parts along dimension 0
The draws below stay inside these ranges and needn't reach their ends.
There are 2 independent parts, one for each index of `groups`. The reference program is written for one: setup_inputs(seed, part) draws one part's arguments, and reference() takes and returns one part's arrays. A program takes and returns all parts, laid end to end along the dimension named above; each array names one. Nothing has to cross between parts.
Inputs may be any that keep to these rules, and one draw needn't show every extreme that they name: `block_mask`: entries are 0 or 1. Let device(b) = b // 2. An entry [a, b] is 1 only where device(b) equals device(a) or device(a) XOR 2**k for k in 0, 1, log2(16) - 2, log2(16) - 1; every diagonal entry is 1. The share of ones differs from one query device to another.
All inputs are finite; a program needn't handle non-finite values.
Results may differ from the reference program's by a relative error of at most 0.03.
Values may be sent and summed in bfloat16 or wider, within the bound.
No kernel may reach another device: no remote copies, remote signals or barrier semaphores. Data moves between devices by JAX's collectives and lax.ppermute only.
A program may use at most 128 MiB of HBM per device.

```python
import jax
import jax.numpy as jnp
from jax import lax

QUERY_HEADS = 20
KEY_VALUE_HEADS = 4
HEAD_SIZE = 128
BLOCK = 128
BLOCKS_DEV = 2
TRAJECTORY_TOKENS = 4096
NB = 32
N_SEQ = 16


def shared_keys(key):
    return jax.random.normal(key, (TRAJECTORY_TOKENS, KEY_VALUE_HEADS, HEAD_SIZE), jnp.float32)


def draw_block_mask(key, part):
    key = jax.random.fold_in(key, 11)
    first, second = jax.random.split(key)
    level = N_SEQ.bit_length() - 1
    blocks = jnp.arange(NB, dtype=jnp.int32)
    owner = blocks // BLOCKS_DEV
    row_dev = owner[:, None]
    col_dev = owner[None, :]
    near = row_dev == col_dev
    for b in (0, 1, level - 2, level - 1):
        near = near | (col_dev == jnp.bitwise_xor(row_dev, 1 << b))
    rate = jax.random.randint(first, (N_SEQ,), 1, 8)
    coin = jax.random.randint(second, (NB, NB), 0, 8)
    chosen_blocks = (coin < rate[owner][:, None]) & near
    chosen_blocks = chosen_blocks | (blocks[:, None] == blocks[None, :])
    return chosen_blocks.astype(jnp.int32)


def draw_keys(key, part):
    base_offset = shared_keys(key)
    return jnp.clip(base_offset, -64.0, 64.0).astype(jnp.bfloat16)


def draw_queries(key, part):
    key = jax.random.fold_in(key, 7)
    first = jax.random.fold_in(key, 0)
    drawn = jax.random.normal(first, (TRAJECTORY_TOKENS, QUERY_HEADS, HEAD_SIZE), jnp.float32)
    return jnp.clip(drawn, -64.0, 64.0).astype(jnp.bfloat16)


def steps_of(stream_key, dims, cuts, smallest, high):
    factor_of = 1.0
    for dim, parts in cuts:
        draws = jax.random.uniform(jax.random.fold_in(jax.random.fold_in(stream_key, 6), dim), (parts,), jnp.float32, smallest / len(cuts), high / len(cuts))
        factor_of = factor_of * jnp.repeat(jnp.exp(draws), dims[dim] // parts).reshape((-1,) + (1,) * (len(dims) - 1 - dim))
    return factor_of


def normal_values(key, dims, scale, bound, shards=(), held_as=jnp.bfloat16):
    array = jax.random.normal(key, dims, jnp.float32) * scale
    if len(shards) > 0:
        array = steps_of(key, dims, shards, -0.22, 0.18) * array
    return jnp.clip(array, min=-bound, max=bound).astype(held_as)


def setup_inputs(seed: int = 0, part: int = 0) -> dict:
    streams_of = jax.random.split(jax.random.key(seed), 6)
    part_keys = jax.random.split(jax.random.fold_in(streams_of[5], part), 6)
    return {
        "block_mask": draw_block_mask(jax.random.fold_in(jax.random.fold_in(streams_of[5], part), 71), part),
        "queries": draw_queries(jax.random.fold_in(jax.random.fold_in(streams_of[5], part), 71), part),
        "keys": draw_keys(jax.random.fold_in(jax.random.fold_in(streams_of[5], part), 71), part),
        "values": normal_values(part_keys[3], (TRAJECTORY_TOKENS, KEY_VALUE_HEADS, HEAD_SIZE), 1.0, 6.0, ((0, 16),)),
        "output_gradient": normal_values(part_keys[4], (TRAJECTORY_TOKENS, QUERY_HEADS, HEAD_SIZE), 1.0, 6.0, ((0, 16),)),
    }


def partner_bits(count):
    level = count.bit_length() - 1
    return (0, 1, level - 2, level - 1)


def product(form, left, right):
    return jnp.einsum(form, left.astype(jnp.float32), right.astype(jnp.float32))


def token_mask(blocks, width):
    return jnp.repeat(jnp.repeat(blocks > 0, width, axis=0), width, axis=1)


def rounded_partial(term):
    return lax.optimization_barrier(term.astype(jnp.bfloat16)).astype(jnp.float32)


def softmax_weights(scores, allowed_mask, top, total):
    masked = jnp.where(allowed_mask, scores, -1e30)
    return (jnp.where(allowed_mask, jnp.exp(masked - top), 0.0) / total).astype(jnp.bfloat16)


def score_grads(dout, value_row_block, weights, delta, softmax_scale):
    dprob = product("qgd,kd->gqk", dout, value_row_block)
    return (weights.astype(jnp.float32) * (dprob - delta) * softmax_scale).astype(jnp.bfloat16)


def attend_single_head(query, dout, key_row_block, value_row_block, allowed_mask, softmax_scale):
    scores = product("qgd,kd->gqk", query, key_row_block) * softmax_scale
    masked = jnp.where(allowed_mask, scores, -1e30)
    top = jnp.max(masked, axis=-1, keepdims=True)
    total = jnp.sum(jnp.where(allowed_mask, jnp.exp(masked - top), 0.0), axis=-1, keepdims=True)
    weights = softmax_weights(scores, allowed_mask, top, total)
    attended = product("gqk,kd->qgd", weights, value_row_block).astype(jnp.bfloat16)
    delta = jnp.sum(dout.astype(jnp.float32) * attended.astype(jnp.float32), axis=-1)
    delta = jnp.transpose(delta)[:, :, None]
    dscore = score_grads(dout, value_row_block, weights, delta, softmax_scale)
    grad_query = product("gqk,kd->qgd", dscore, key_row_block).astype(jnp.bfloat16)
    key_gradient = product("gqk,qgd->kd", dscore, query)
    value_gradient = product("gqk,qgd->kd", weights, dout)
    return attended, grad_query, key_gradient, value_gradient


def reference(block_mask, queries, keys, values, output_gradient):
    softmax_scale = HEAD_SIZE ** -0.5
    head_group = QUERY_HEADS // KEY_VALUE_HEADS
    per_partition = BLOCKS_DEV * BLOCK
    bits = partner_bits(N_SEQ)
    devices = jnp.arange(N_SEQ, dtype=jnp.int32)
    sources = jnp.stack([devices] + [jnp.bitwise_xor(devices, 1 << b) for b in bits], axis=1)
    query_local = queries.reshape(N_SEQ, per_partition, KEY_VALUE_HEADS, head_group, HEAD_SIZE)
    output_gradient_local = output_gradient.reshape(N_SEQ, per_partition, KEY_VALUE_HEADS, head_group, HEAD_SIZE)
    key_local = keys.reshape(N_SEQ, per_partition, KEY_VALUE_HEADS, HEAD_SIZE)
    value_local = values.reshape(N_SEQ, per_partition, KEY_VALUE_HEADS, HEAD_SIZE)
    mask_dev = block_mask.reshape(N_SEQ, BLOCKS_DEV, N_SEQ, BLOCKS_DEV)

    def one_device(block_index):
        chosen_blocks = sources[block_index]
        key_row_block = key_local[chosen_blocks].reshape(5 * per_partition, KEY_VALUE_HEADS, HEAD_SIZE)
        value_row_block = value_local[chosen_blocks].reshape(5 * per_partition, KEY_VALUE_HEADS, HEAD_SIZE)
        blocks = mask_dev[block_index][:, chosen_blocks, :].reshape(BLOCKS_DEV, 5 * BLOCKS_DEV)
        allowed_mask = token_mask(blocks, BLOCK)[None]
        collected_results = [attend_single_head(query_local[block_index][:, head_number], output_gradient_local[block_index][:, head_number], key_row_block[:, head_number], value_row_block[:, head_number], allowed_mask, softmax_scale) for head_number in range(KEY_VALUE_HEADS)]
        return tuple(jnp.stack([r[k] for r in collected_results], axis=1) for k in range(4))

    attended, grad_query, key_partial_sums, value_partial_sums = lax.map(one_device, devices)
    key_partial_sums = rounded_partial(key_partial_sums).reshape(N_SEQ, 5, per_partition, KEY_VALUE_HEADS, HEAD_SIZE)
    value_partial_sums = rounded_partial(value_partial_sums).reshape(N_SEQ, 5, per_partition, KEY_VALUE_HEADS, HEAD_SIZE)
    key_gradient = key_partial_sums[:, 0]
    value_gradient = value_partial_sums[:, 0]
    for slot in range(1, 5):
        key_gradient = key_gradient + key_partial_sums[sources[:, slot], slot]
        value_gradient = value_gradient + value_partial_sums[sources[:, slot], slot]
    return (attended.reshape(TRAJECTORY_TOKENS, QUERY_HEADS, HEAD_SIZE), grad_query.reshape(TRAJECTORY_TOKENS, QUERY_HEADS, HEAD_SIZE),
            key_gradient.reshape(TRAJECTORY_TOKENS, KEY_VALUE_HEADS, HEAD_SIZE).astype(jnp.bfloat16), value_gradient.reshape(TRAJECTORY_TOKENS, KEY_VALUE_HEADS, HEAD_SIZE).astype(jnp.bfloat16))
```

```python
import functools

import jax
import jax.numpy as jnp
from jax import lax
from jax.experimental import pallas as pl
from jax.experimental.pallas import tpu as pltpu
from jax.sharding import PartitionSpec as P

LOG2E = 1.4426950408889634
MASKED = -1e30
CHUNKS = 2
VMEM_LIMIT = 48 * 2**20


def from_partner(value, axis, apart):
    mask = 2**apart
    pairs = [(source, source ^ mask) for source in range(lax.axis_size(axis))]
    return lax.ppermute(value, axis, pairs)


def partner_bits(count):
    level = count.bit_length() - 1
    return (0, 1, level - 2, level - 1)


def product(left, right):
    return lax.dot_general(left, right, (((1,), (0,)), ((), ())), preferred_element_type=jnp.float32)


def product_nt(left, right):
    return lax.dot_general(left, right, (((1,), (1,)), ((), ())), preferred_element_type=jnp.float32)


def attend_kernel(head_group, rows, width, softmax_scale, bits, me_ref, mask_ref, q_ref, do_ref, *refs):
    sources = len(bits) + 1
    kv_refs = refs[:sources]
    o_ref, dq_ref = refs[sources : sources + 2]
    term_refs = refs[sources + 2 : 2 * sources + 2]
    dk_ref, dv_ref = refs[2 * sources + 2 :]
    scale2 = softmax_scale * LOG2E
    me = me_ref[0]
    devices = [me] + [jnp.bitwise_xor(me, 1 << bit) for bit in bits]
    bias = [
        [[jnp.where(mask_ref[a, device * rows + b] > 0, 0.0, MASKED) for b in range(rows)] for a in range(rows)]
        for device in devices
    ]

    def biased(x, s):
        return jnp.concatenate(
            [
                jnp.concatenate(
                    [x[a * width : (a + 1) * width, b * width : (b + 1) * width] + bias[s][a][b] for b in range(rows)],
                    axis=1,
                )
                for a in range(rows)
            ],
            axis=0,
        )

    for g in range(head_group):
        q = q_ref[g]
        do = do_ref[g]
        scores = [biased(product_nt(q, kv_refs[s][0, 0]), s) for s in range(sources)]
        top = jnp.max(functools.reduce(jnp.maximum, scores), axis=1, keepdims=True) * scale2
        exps = [jnp.exp2(x * scale2 - top) for x in scores]
        total = jnp.sum(functools.reduce(jnp.add, exps), axis=1, keepdims=True)
        inverse = 1.0 / total
        narrow = [e.astype(jnp.bfloat16) for e in exps]
        attended = functools.reduce(jnp.add, [product(narrow[s], kv_refs[s][1, 0]) for s in range(sources)])
        attended = (attended * inverse).astype(jnp.bfloat16)
        o_ref[g] = attended
        wide_do = do.astype(jnp.float32)
        delta = jnp.sum(wide_do * attended.astype(jnp.float32), axis=1, keepdims=True)
        q_scaled = (q.astype(jnp.float32) * (inverse * softmax_scale)).astype(jnp.bfloat16).T
        do_scaled = (wide_do * inverse).astype(jnp.bfloat16).T
        grad_q = 0.0
        for s in range(sources):
            dprob = product_nt(do, kv_refs[s][1, 0])
            dscore = (exps[s] * (dprob - delta)).astype(jnp.bfloat16)
            grad_q = grad_q + product(dscore, kv_refs[s][0, 0])
            dk = product(q_scaled, dscore)
            dv = product(do_scaled, narrow[s])
            if g == 0:
                dk_ref[s] = dk
                dv_ref[s] = dv
            else:
                dk_ref[s] += dk
                dv_ref[s] += dv
        dq_ref[g] = (grad_q * (inverse * softmax_scale)).astype(jnp.bfloat16)
    for s in range(sources):
        term_refs[s][0, 0] = dk_ref[s].T.astype(jnp.bfloat16)
        term_refs[s][1, 0] = dv_ref[s].T.astype(jnp.bfloat16)


def attend(me, block_mask, queries, output_gradient, kvs, first, width, bits):
    heads_all, tokens, size = queries.shape
    n = kvs[0].shape[1]
    head_group = heads_all // (CHUNKS * n)
    sources = len(kvs)
    rows = block_mask.shape[0]
    rows_in = pl.BlockSpec((head_group, tokens, size), lambda j: (first + j, 0, 0))
    rows_out = pl.BlockSpec((head_group, tokens, size), lambda j: (j, 0, 0))
    term = pl.BlockSpec((2, 1, tokens, size), lambda j: (0, j, 0, 0))
    smem = pl.BlockSpec(memory_space=pltpu.SMEM)
    out = jax.ShapeDtypeStruct((n * head_group, tokens, size), jnp.bfloat16)
    term_out = jax.ShapeDtypeStruct((2, n, tokens, size), jnp.bfloat16)
    body = functools.partial(attend_kernel, head_group, rows, width, size ** (-0.5), bits)
    scores = n * head_group * tokens * sources * tokens
    return pl.pallas_call(
        body,
        grid=(n,),
        in_specs=[smem, smem, rows_in, rows_in] + [term] * sources,
        out_specs=[rows_out, rows_out] + [term] * sources,
        out_shape=[out, out] + [term_out] * sources,
        scratch_shapes=[pltpu.VMEM((sources, size, tokens), jnp.float32)] * 2,
        compiler_params=pltpu.CompilerParams(vmem_limit_bytes=VMEM_LIMIT),
        cost_estimate=pl.CostEstimate(
            flops=12 * scores * size, bytes_accessed=8 * n * head_group * tokens * size, transcendentals=scores
        ),
    )(me, block_mask, queries, output_gradient, *kvs)


def shards(block_mask, queries, keys, values, output_gradient):
    count = lax.axis_size("seq")
    me = lax.axis_index("seq").astype(jnp.int32).reshape(1)
    width = queries.shape[0] // block_mask.shape[0]
    kv_heads = keys.shape[1]
    bits = partner_bits(count)
    q = jnp.transpose(queries, (1, 0, 2))
    dout = jnp.transpose(output_gradient, (1, 0, 2))
    per = kv_heads // CHUNKS
    own = [
        jnp.stack([jnp.transpose(x[:, c * per : (c + 1) * per], (1, 0, 2)) for x in (keys, values)])
        for c in range(CHUNKS)
    ]
    fetched = [[own[c]] + [from_partner(own[c], "seq", bit) for bit in bits] for c in range(CHUNKS)]
    results = [attend(me, block_mask, q, dout, fetched[c], c * per, width, bits) for c in range(CHUNKS)]
    grads = []
    for c in range(CHUNKS):
        terms = results[c][2:]
        total = terms[0].astype(jnp.float32)
        for bit, term in zip(bits, terms[1:]):
            total = total + from_partner(term, "seq", bit).astype(jnp.float32)
        grads.append(total.astype(jnp.bfloat16))
    both = jnp.concatenate(grads, axis=1)
    attended = jnp.transpose(jnp.concatenate([r[0] for r in results], axis=0), (1, 0, 2))
    grad_q = jnp.transpose(jnp.concatenate([r[1] for r in results], axis=0), (1, 0, 2))
    return (attended, grad_q, jnp.transpose(both[0], (1, 0, 2)), jnp.transpose(both[1], (1, 0, 2)))


def solution(mesh):
    rows = P(("groups", "seq"), None)
    cube = P(("groups", "seq"), None, None)
    return jax.shard_map(
        shards,
        mesh=mesh,
        in_specs=(rows, cube, cube, cube, cube),
        out_specs=(cube, cube, cube, cube),
        check_vma=False,
    )
```

```python
import functools

import jax
import jax.numpy as jnp
from jax import lax
from jax.experimental import pallas as pl
from jax.experimental.pallas import tpu as pltpu
from jax.sharding import PartitionSpec as P

LOG2E = 1.4426950408889634
MASKED = -1e30
VMEM_LIMIT = 24 * 2**20
FETCH = (((0, 4),), ((0, 4),), ((0, 2), (2, 4)), ((0, 2), (2, 4)))
RETURN = (((0, 4),), ((0, 4),), ((0, 2), (2, 4)), ((0, 2), (2, 4)))
KERNELS = ((0, 2), (2, 4))


def from_partner(value, axis, apart):
    mask = 2**apart
    pairs = [(source, source ^ mask) for source in range(lax.axis_size(axis))]
    return lax.ppermute(value, axis, pairs)


def partner_bits(count):
    level = count.bit_length() - 1
    return (0, 1, level - 2, level - 1)


def group_of(groups, head):
    return next(g for g in groups if g[0] <= head < g[1])


def product(left, right):
    return lax.dot_general(left, right, (((1,), (0,)), ((), ())), preferred_element_type=jnp.float32)


def product_nt(left, right):
    return lax.dot_general(left, right, (((1,), (1,)), ((), ())), preferred_element_type=jnp.float32)


VMEM = pl.BlockSpec(memory_space=pltpu.VMEM)
SMEM = pl.BlockSpec(memory_space=pltpu.SMEM)
ANY = pl.BlockSpec(memory_space=pl.ANY)
HBM = pl.BlockSpec(memory_space=pltpu.HBM)


def in_hbm(array):
    return pltpu.with_memory_space_constraint(array, pltpu.HBM)


def pack_kernel(groups, bits, me_ref, mask_ref, k_ref, v_ref, bias_ref, *refs):
    outs, wide_ref = refs[:-1], refs[-1]
    tokens, heads, size = k_ref.shape
    for i, ref in enumerate((k_ref, v_ref)):
        wide_ref[i] = ref[...].astype(jnp.float32).reshape(tokens * heads, size)
        for h in range(heads):
            rows = wide_ref[i, pl.ds(h, tokens, stride=heads), :].astype(jnp.bfloat16)
            for (low, high), out in zip(groups, outs):
                if low <= h < high:
                    out[h - low, i] = rows
    me = me_ref[0]
    blocks, columns = mask_ref.shape
    mask = mask_ref[...]
    column = lax.broadcasted_iota(jnp.int32, (blocks, columns), 1)
    for s, device in enumerate([me] + [jnp.bitwise_xor(me, 1 << bit) for bit in bits]):
        for b in range(blocks):
            ones = jnp.sum(jnp.where(column == device * blocks + b, mask, 0), axis=1, keepdims=True)
            width = tokens // blocks
            bias_ref[s, :, b * width : (b + 1) * width] = jnp.broadcast_to(
                jnp.where(ones > 0, 0.0, MASKED), (blocks, width)
            )


def pack(me, block_mask, keys, values, groups, bits):
    tokens, heads, size = keys.shape
    bias = jax.ShapeDtypeStruct((len(bits) + 1, block_mask.shape[0], tokens), jnp.float32)
    return pl.pallas_call(
        functools.partial(pack_kernel, groups, bits),
        in_specs=[SMEM] + [VMEM] * 3,
        out_specs=[VMEM] * (len(groups) + 1),
        out_shape=[bias]
        + [jax.ShapeDtypeStruct((high - low, 2, tokens, size), keys.dtype) for low, high in groups],
        scratch_shapes=[pltpu.VMEM((2, tokens * heads, size), jnp.float32)],
        compiler_params=pltpu.CompilerParams(vmem_limit_bytes=VMEM_LIMIT),
        cost_estimate=pl.CostEstimate(flops=0, bytes_accessed=6 * keys.size * 2, transcendentals=0),
    )(me, in_hbm(block_mask), in_hbm(keys), in_hbm(values))


def sum_kernel(groups, *refs):
    terms, (dk_ref, dv_ref, wide_ref) = refs[: len(groups)], refs[len(groups) :]
    tokens, heads, size = dk_ref.shape
    for i, ref in enumerate((dk_ref, dv_ref)):
        for h in range(heads):
            parts = [t[h - g[0], i].astype(jnp.float32) for g, t in zip(groups, terms) if g[0] <= h < g[1]]
            wide_ref[i, pl.ds(h, tokens, stride=heads), :] = functools.reduce(jnp.add, parts)
        ref[...] = wide_ref[i].astype(ref.dtype).reshape(tokens, heads, size)


def sum_terms(groups, terms, tokens, heads, size):
    out = jax.ShapeDtypeStruct((tokens, heads, size), jnp.bfloat16)
    return pl.pallas_call(
        functools.partial(sum_kernel, groups),
        in_specs=[VMEM] * len(groups),
        out_specs=[VMEM] * 2,
        out_shape=[out, out],
        scratch_shapes=[pltpu.VMEM((2, tokens * heads, size), jnp.float32)],
        compiler_params=pltpu.CompilerParams(vmem_limit_bytes=VMEM_LIMIT),
        cost_estimate=pl.CostEstimate(flops=0, bytes_accessed=12 * tokens * heads * size * 2, transcendentals=0),
    )(*terms)


def attend_kernel(sources, softmax_scale, unused, bias_ref, q_ref, do_ref, *refs):
    kv_refs = refs[:sources]
    refs = refs[sources + unused :]
    o_ref, dq_ref = refs[:2]
    term_refs = refs[2 : sources + 2]
    dk_ref, dv_ref, x_ref, e_ref, p_ref = refs[sources + 2 :]
    scale2 = softmax_scale * LOG2E
    blocks = bias_ref.shape[1]
    width = bias_ref.shape[2] // blocks
    head_group = q_ref.shape[0]
    state = {}

    def key(s):
        return kv_refs[s][0, 0]

    def value(s):
        return kv_refs[s][0, 1]

    def scores(g, s):
        x = product_nt(q_ref[g], key(s))
        x = jnp.concatenate([x[a * width : (a + 1) * width] + bias_ref[s, a : a + 1] for a in range(blocks)], axis=0)
        x_ref[g % 2, s] = x
        state["max", g] = jnp.maximum(state["max", g], x) if s else x
        p_ref[g % 2, s] = product_nt(do_ref[g], value(s))

    def scores_end(g):
        state["top", g] = jnp.max(state.pop(("max", g)), axis=1, keepdims=True) * scale2

    def forward(g, s):
        e = jnp.exp2(x_ref[g % 2, s] * scale2 - state["top", g])
        narrow = e.astype(jnp.bfloat16)
        e_ref[g % 2, s] = narrow
        state["total", g] = state["total", g] + e if s else e
        part = product(narrow, value(s))
        state["out", g] = state["out", g] + part if s else part

    def forward_end(g):
        q, do = q_ref[g], do_ref[g].astype(jnp.float32)
        inverse = 1.0 / jnp.sum(state.pop(("total", g)), axis=1, keepdims=True)
        attended = (state.pop(("out", g)) * inverse).astype(jnp.bfloat16)
        o_ref[g] = attended
        state["delta", g] = jnp.sum(do * attended.astype(jnp.float32), axis=1, keepdims=True)
        state["q", g] = (q.astype(jnp.float32) * (inverse * softmax_scale)).astype(jnp.bfloat16).T
        state["do", g] = (do * inverse).astype(jnp.bfloat16).T
        state["scale", g] = inverse * softmax_scale

    def backward(g, s):
        e = e_ref[g % 2, s]
        dv = product(state["do", g], e)
        dscore = (e.astype(jnp.float32) * (p_ref[g % 2, s] - state["delta", g])).astype(jnp.bfloat16)
        part = product(dscore, key(s))
        state["dq", g] = state["dq", g] + part if s else part
        dk = product(state["q", g], dscore)
        if g == 0:
            dk_ref[s] = dk
            dv_ref[s] = dv
        elif g < head_group - 1:
            dk_ref[s] += dk
            dv_ref[s] += dv
        else:
            term_refs[s][0, 0] = (dk_ref[s] + dk).T.astype(jnp.bfloat16)
            term_refs[s][0, 1] = (dv_ref[s] + dv).T.astype(jnp.bfloat16)

    def backward_end(g):
        dq_ref[g] = (state.pop(("dq", g)) * state["scale", g]).astype(jnp.bfloat16)

    every = range(sources)
    for s in every:
        scores(0, s)
    scores_end(0)
    for g in range(head_group):
        for s in every:
            forward(g, s)
            if g:
                backward(g - 1, s)
        if g:
            backward_end(g - 1)
        if g + 1 < head_group:
            for s in every:
                scores(g + 1, s)
        forward_end(g)
        if g + 1 < head_group:
            scores_end(g + 1)
    for s in every:
        backward(head_group - 1, s)
    backward_end(head_group - 1)

def attend(heads, head_group, bias, queries, output_gradient, kvs, outs, after):
    heads_all, tokens, size = queries.shape
    sources = len(kvs)
    first, last = heads
    rows = pl.BlockSpec((head_group, tokens, size), lambda j: (first + j, 0, 0))

    def block(begin):
        return pl.BlockSpec((1, 2, tokens, size), lambda j: (first - begin + j, 0, 0, 0))

    shapes = [(heads_all, tokens, size)] * 2 + [(g[1] - g[0], 2, tokens, size) for _, g in outs[2:]]
    chained = [(n, a) for n, (a, _) in enumerate(outs) if a is not None]
    scores = (last - first) * head_group * tokens * sources * tokens
    return pl.pallas_call(
        functools.partial(attend_kernel, sources, size ** (-0.5), len(chained) + len(after)),
        grid=(last - first,),
        in_specs=[VMEM, rows, rows] + [block(begin) for _, begin in kvs] + [ANY] * (len(chained) + len(after)),
        out_specs=[rows, rows] + [block(g[0]) for _, g in outs[2:]],
        out_shape=[jax.ShapeDtypeStruct(s, jnp.bfloat16) for s in shapes],
        scratch_shapes=[pltpu.VMEM((sources, size, tokens), jnp.float32)] * 2
        + [
            pltpu.VMEM((2, sources, tokens, tokens), jnp.float32),
            pltpu.VMEM((2, sources, tokens, tokens), jnp.bfloat16),
            pltpu.VMEM((2, sources, tokens, tokens), jnp.float32),
        ],
        input_output_aliases={3 + sources + i: n for i, (n, _) in enumerate(chained)},
        compiler_params=pltpu.CompilerParams(vmem_limit_bytes=VMEM_LIMIT),
        cost_estimate=pl.CostEstimate(
            flops=12 * scores * size,
            bytes_accessed=8 * (last - first) * head_group * tokens * size,
            transcendentals=scores,
        ),
    )(bias, in_hbm(queries), in_hbm(output_gradient), *[a for a, _ in kvs], *[a for _, a in chained], *after)


def shards(block_mask, queries, keys, values, output_gradient):
    count = lax.axis_size("seq")
    me = lax.axis_index("seq").astype(jnp.int32).reshape(1)
    tokens, kv_heads, size = keys.shape
    head_group = queries.shape[1] // kv_heads
    bits = partner_bits(count)
    q = jnp.transpose(queries, (1, 0, 2))
    dout = jnp.transpose(output_gradient, (1, 0, 2))
    whole = (0, kv_heads)
    groups = sorted({g for slot in FETCH for g in slot} | {whole})
    bias, *arrays = pack(me, block_mask, keys, values, groups, bits)
    packed = dict(zip(groups, arrays))
    fetched = [
        {group: from_partner(packed[group], "seq", bit) for group in slot} for bit, slot in zip(bits, FETCH)
    ]
    made = {}
    returned = {}
    for heads in KERNELS:
        kvs = [(packed[whole], 0)]
        for slot, got in zip(FETCH, fetched):
            group = group_of(slot, heads[0])
            kvs.append((got[group], group[0]))
        spots = [("o", whole), ("dq", whole), ("own", whole)]
        spots += [(slot, group_of(RETURN[slot], heads[0])) for slot in range(len(bits))]
        outs = [(made.get(spot), spot[1]) for spot in spots]
        results = attend(heads, head_group, bias, q, dout, kvs, outs, [])
        made.update(zip(spots, results))
        before = list(returned.values())
        for slot in reversed(range(len(bits))):
            for group in RETURN[slot]:
                if group[1] == heads[1]:
                    term = made[slot, group]
                    if before:
                        term = lax.optimization_barrier((term, *before))[0]
                    returned[slot, group] = from_partner(term, "seq", bits[slot])
    term_groups = [whole] + [group for _, group in returned]
    terms = [made["own", whole]] + list(returned.values())
    grad_keys, grad_values = sum_terms(term_groups, terms, tokens, kv_heads, size)
    attended = made["o", whole]
    grad_queries = made["dq", whole]
    return (jnp.transpose(attended, (1, 0, 2)), jnp.transpose(grad_queries, (1, 0, 2)), grad_keys, grad_values)


def solution(mesh):
    rows = P(("groups", "seq"), None)
    cube = P(("groups", "seq"), None, None)
    return jax.shard_map(
        shards,
        mesh=mesh,
        in_specs=(rows, cube, cube, cube, cube),
        out_specs=(cube, cube, cube, cube),
        check_vma=False,
    )
```

```python
import functools

import jax
import jax.numpy as jnp
from jax import lax
from jax.experimental import pallas as pl
from jax.experimental.pallas import tpu as pltpu
from jax.sharding import PartitionSpec as P

LOG2E = 1.4426950408889634
MASKED = -1e30
VMEM_LIMIT = 24 * 2**20
LOCAL = (0, 1)
REMOTE = (2, 3, 4)
HALVES = ((0, 2), (2, 4))


def from_partner(value, axis, apart):
    mask = 2**apart
    pairs = [(source, source ^ mask) for source in range(lax.axis_size(axis))]
    return lax.ppermute(value, axis, pairs)


def partner_bits(count):
    level = count.bit_length() - 1
    return (0, 1, level - 2, level - 1)


def product(left, right):
    return lax.dot_general(left, right, (((1,), (0,)), ((), ())), preferred_element_type=jnp.float32)


def product_nt(left, right):
    return lax.dot_general(left, right, (((1,), (1,)), ((), ())), preferred_element_type=jnp.float32)


VMEM = pl.BlockSpec(memory_space=pltpu.VMEM)
SMEM = pl.BlockSpec(memory_space=pltpu.SMEM)
ANY = pl.BlockSpec(memory_space=pl.ANY)


def in_hbm(array):
    return pltpu.with_memory_space_constraint(array, pltpu.HBM)


def pack_kernel(groups, bits, me_ref, mask_ref, k_ref, v_ref, bias_ref, *refs):
    outs, wide_ref = refs[:-1], refs[-1]
    tokens, heads, size = k_ref.shape
    for i, ref in enumerate((k_ref, v_ref)):
        wide_ref[i] = ref[...].astype(jnp.float32).reshape(tokens * heads, size)
        for h in range(heads):
            rows = wide_ref[i, pl.ds(h, tokens, stride=heads), :].astype(jnp.bfloat16)
            for (low, high), out in zip(groups, outs):
                if low <= h < high:
                    out[h - low, i] = rows
    me = me_ref[0]
    blocks, columns = mask_ref.shape
    mask = mask_ref[...]
    column = lax.broadcasted_iota(jnp.int32, (blocks, columns), 1)
    for s, device in enumerate([me] + [jnp.bitwise_xor(me, 1 << bit) for bit in bits]):
        for b in range(blocks):
            ones = jnp.sum(jnp.where(column == device * blocks + b, mask, 0), axis=1, keepdims=True)
            width = tokens // blocks
            bias_ref[s, :, b * width : (b + 1) * width] = jnp.broadcast_to(
                jnp.where(ones > 0, 0.0, MASKED), (blocks, width)
            )


def pack(me, block_mask, keys, values, groups, bits):
    tokens, heads, size = keys.shape
    bias = jax.ShapeDtypeStruct((len(bits) + 1, block_mask.shape[0], tokens), jnp.float32)
    return pl.pallas_call(
        functools.partial(pack_kernel, groups, bits),
        in_specs=[SMEM] + [VMEM] * 3,
        out_specs=[VMEM] * (len(groups) + 1),
        out_shape=[bias]
        + [jax.ShapeDtypeStruct((high - low, 2, tokens, size), keys.dtype) for low, high in groups],
        scratch_shapes=[pltpu.VMEM((2, tokens * heads, size), jnp.float32)],
        compiler_params=pltpu.CompilerParams(vmem_limit_bytes=VMEM_LIMIT),
        cost_estimate=pl.CostEstimate(flops=0, bytes_accessed=6 * keys.size * 2, transcendentals=0),
    )(me, in_hbm(block_mask), in_hbm(keys), in_hbm(values))


def gather_kernel(groups, *refs):
    terms, out = refs[:-1], refs[-1]
    for h in range(out.shape[0]):
        parts = [t[h - g[0]].astype(jnp.float32) for g, t in zip(groups, terms) if g[0] <= h < g[1]]
        out[h] = functools.reduce(jnp.add, parts)


def gather_terms(groups, terms, heads):
    return pl.pallas_call(
        functools.partial(gather_kernel, groups),
        in_specs=[VMEM] * len(groups),
        out_specs=VMEM,
        out_shape=jax.ShapeDtypeStruct((heads,) + terms[0].shape[1:], jnp.float32),
        compiler_params=pltpu.CompilerParams(vmem_limit_bytes=VMEM_LIMIT),
        cost_estimate=pl.CostEstimate(flops=0, bytes_accessed=8 * 2**20, transcendentals=0),
    )(*terms)


def sum_kernel(groups, *refs):
    terms, (dk_ref, dv_ref, wide_ref) = refs[: len(groups)], refs[len(groups) :]
    tokens, heads, size = dk_ref.shape
    for i, ref in enumerate((dk_ref, dv_ref)):
        for h in range(heads):
            parts = [t[h - g[0], i].astype(jnp.float32) for g, t in zip(groups, terms) if g[0] <= h < g[1]]
            wide_ref[i, pl.ds(h, tokens, stride=heads), :] = functools.reduce(jnp.add, parts)
        ref[...] = wide_ref[i].astype(ref.dtype).reshape(tokens, heads, size)


def sum_terms(groups, terms, tokens, heads, size):
    out = jax.ShapeDtypeStruct((tokens, heads, size), jnp.bfloat16)
    return pl.pallas_call(
        functools.partial(sum_kernel, groups),
        in_specs=[VMEM] * len(groups),
        out_specs=[VMEM] * 2,
        out_shape=[out, out],
        scratch_shapes=[pltpu.VMEM((2, tokens * heads, size), jnp.float32)],
        compiler_params=pltpu.CompilerParams(vmem_limit_bytes=VMEM_LIMIT),
        cost_estimate=pl.CostEstimate(flops=0, bytes_accessed=12 * tokens * heads * size * 2, transcendentals=0),
    )(*terms)


def scores_of(q, key, bias_ref, s):
    x = product_nt(q, key)
    blocks = bias_ref.shape[1]
    width = x.shape[0] // blocks
    return jnp.concatenate([x[a * width : (a + 1) * width] + bias_ref[s, a : a + 1] for a in range(blocks)], axis=0)


def pair(first, second, shape):
    lane = lax.broadcasted_iota(jnp.int32, shape, 1)
    return jnp.where(lane < shape[1] // 2, first, second)


def unpair(array):
    half = array.shape[1] // 2
    return array[:, 0:1], array[:, half : half + 1]


def local_kernel(softmax_scale, bias_ref, q_ref, *refs):
    sources = len(LOCAL)
    kv_refs = refs[:sources]
    e_ref, o_ref, stat_ref, x_ref = refs[sources:]
    scale2 = softmax_scale * LOG2E
    head_group, tokens, size = q_ref.shape
    state = {}

    def scores(g, n):
        x = scores_of(q_ref[g], kv_refs[n][0, 0], bias_ref, LOCAL[n])
        x_ref[g % 2, n] = x
        state["max", g] = jnp.maximum(state["max", g], x) if n else x

    def scores_end(g):
        state["top", g] = jnp.max(state.pop(("max", g)), axis=1, keepdims=True) * scale2

    def forward(g, n):
        e = jnp.exp2(x_ref[g % 2, n] * scale2 - state["top", g])
        narrow = e.astype(jnp.bfloat16)
        e_ref[g, n] = narrow
        state["total", g] = state["total", g] + e if n else e
        part = product(narrow, kv_refs[n][0, 1])
        state["out", g] = state["out", g] + part if n else part

    def forward_end(g):
        o_ref[g] = state.pop(("out", g))
        total = jnp.sum(state.pop(("total", g)), axis=1, keepdims=True)
        stat_ref[g] = pair(state["top", g], total, (tokens, size))

    every = range(sources)
    for n in every:
        scores(0, n)
    scores_end(0)
    for g in range(head_group):
        for n in every:
            forward(g, n)
            if g + 1 < head_group:
                scores(g + 1, n)
        forward_end(g)
        if g + 1 < head_group:
            scores_end(g + 1)


def remote_kernel(softmax_scale, unused, bias_ref, q_ref, do_ref, part_ref, stat_ref, *refs):
    sources = len(REMOTE)
    kv_refs = refs[:sources]
    refs = refs[sources + unused :]
    o_ref, dq_ref, row_ref = refs[:3]
    term_refs = refs[3 : sources + 3]
    dk_ref, dv_ref, x_ref, e_ref, p_ref = refs[sources + 3 :]
    scale2 = softmax_scale * LOG2E
    head_group, tokens, size = q_ref.shape
    state = {}

    def key(n):
        return kv_refs[n][0, 0]

    def value(n):
        return kv_refs[n][0, 1]

    def scores(g, n):
        x = scores_of(q_ref[g], key(n), bias_ref, REMOTE[n])
        x_ref[g % 2, n] = x
        state["max", g] = jnp.maximum(state["max", g], x) if n else x
        p_ref[g % 2, n] = product_nt(do_ref[g], value(n))

    def scores_end(g):
        local, total = unpair(stat_ref[g])
        top = jnp.maximum(jnp.max(state.pop(("max", g)), axis=1, keepdims=True) * scale2, local)
        state["top", g] = top
        state["share", g] = jnp.exp2(local - top)
        state["part", g] = total * state["share", g]

    def forward(g, n):
        e = jnp.exp2(x_ref[g % 2, n] * scale2 - state["top", g])
        narrow = e.astype(jnp.bfloat16)
        e_ref[g % 2, n] = narrow
        state["total", g] = state["total", g] + e if n else e
        part = product(narrow, value(n))
        state["out", g] = state["out", g] + part if n else part

    def forward_end(g):
        q, do = q_ref[g], do_ref[g].astype(jnp.float32)
        total = jnp.sum(state.pop(("total", g)), axis=1, keepdims=True) + state["part", g]
        inverse = 1.0 / total
        attended = state.pop(("out", g)) + part_ref[g] * state["share", g]
        attended = (attended * inverse).astype(jnp.bfloat16)
        o_ref[g] = attended
        delta = jnp.sum(do * attended.astype(jnp.float32), axis=1, keepdims=True)
        state["delta", g] = delta
        row_ref[g] = pair(state["share", g] * inverse, delta, (tokens, size))
        state["q", g] = (q.astype(jnp.float32) * (inverse * softmax_scale)).astype(jnp.bfloat16).T
        state["do", g] = (do * inverse).astype(jnp.bfloat16).T
        state["scale", g] = inverse * softmax_scale

    def backward(g, n):
        e = e_ref[g % 2, n]
        dv = product(state["do", g], e)
        dscore = (e.astype(jnp.float32) * (p_ref[g % 2, n] - state["delta", g])).astype(jnp.bfloat16)
        part = product(dscore, key(n))
        state["dq", g] = state["dq", g] + part if n else part
        dk = product(state["q", g], dscore)
        if g == 0:
            dk_ref[n] = dk
            dv_ref[n] = dv
        elif g < head_group - 1:
            dk_ref[n] += dk
            dv_ref[n] += dv
        else:
            term_refs[n][0, 0] = (dk_ref[n] + dk).T.astype(jnp.bfloat16)
            term_refs[n][0, 1] = (dv_ref[n] + dv).T.astype(jnp.bfloat16)

    def backward_end(g):
        dq_ref[g] = state.pop(("dq", g)) * state["scale", g]

    every = range(sources)
    for n in every:
        scores(0, n)
    scores_end(0)
    for g in range(head_group):
        for n in every:
            forward(g, n)
            if g:
                backward(g - 1, n)
        if g:
            backward_end(g - 1)
        if g + 1 < head_group:
            for n in every:
                scores(g + 1, n)
        forward_end(g)
        if g + 1 < head_group:
            scores_end(g + 1)
    for n in every:
        backward(head_group - 1, n)
    backward_end(head_group - 1)


def rest_kernel(softmax_scale, unused, q_ref, do_ref, e_ref, part_ref, row_ref, *refs):
    sources = len(LOCAL)
    kv_refs = refs[:sources]
    refs = refs[sources + unused :]
    dq_ref = refs[0]
    term_refs = refs[1 : sources + 1]
    dk_ref, dv_ref, p_ref = refs[sources + 1 :]
    head_group = q_ref.shape[0]
    state = {}

    def dprob(g, n):
        p_ref[g % 2, n] = product_nt(do_ref[g], kv_refs[n][0, 1])

    def rows(g):
        share, delta = unpair(row_ref[g])
        state["delta", g] = delta
        state["scale", g] = share * softmax_scale
        state["q", g] = (q_ref[g].astype(jnp.float32) * state["scale", g]).astype(jnp.bfloat16).T
        state["do", g] = (do_ref[g].astype(jnp.float32) * share).astype(jnp.bfloat16).T

    def backward(g, n):
        e = e_ref[g, n]
        dv = product(state["do", g], e)
        dscore = (e.astype(jnp.float32) * (p_ref[g % 2, n] - state["delta", g])).astype(jnp.bfloat16)
        part = product(dscore, kv_refs[n][0, 0])
        state["dq", g] = state["dq", g] + part if n else part
        dk = product(state["q", g], dscore)
        if g == 0:
            dk_ref[n] = dk
            dv_ref[n] = dv
        elif g < head_group - 1:
            dk_ref[n] += dk
            dv_ref[n] += dv
        else:
            term_refs[n][0, 0] = (dk_ref[n] + dk).T.astype(jnp.bfloat16)
            term_refs[n][0, 1] = (dv_ref[n] + dv).T.astype(jnp.bfloat16)

    every = range(sources)
    for n in every:
        dprob(0, n)
    rows(0)
    for g in range(head_group):
        for n in every:
            backward(g, n)
            if g + 1 < head_group:
                dprob(g + 1, n)
        dq_ref[g] = (part_ref[g] + state.pop(("dq", g)) * state["scale", g]).astype(jnp.bfloat16)
        if g + 1 < head_group:
            rows(g + 1)


def cost(products, heads, head_group, tokens, sources, size):
    scores = heads * head_group * tokens * tokens * sources
    return pl.CostEstimate(
        flops=2 * products * scores * size,
        bytes_accessed=8 * heads * head_group * tokens * size,
        transcendentals=scores,
    )


def attend(bias, queries, output_gradient, heads_all, head_group):
    tokens, size = queries.shape[1:]

    def rows(first):
        return pl.BlockSpec((head_group, tokens, size), lambda j: (first + j, 0, 0))

    def block(first, begin):
        return pl.BlockSpec((1, 2, tokens, size), lambda j: (first - begin + j, 0, 0, 0))

    def exps(first):
        return pl.BlockSpec((head_group, len(LOCAL), tokens, tokens), lambda j: (first + j, 0, 0, 0))

    scale = size ** (-0.5)
    query_heads = heads_all * head_group
    wide = jax.ShapeDtypeStruct((query_heads, tokens, size), jnp.float32)
    narrow = jax.ShapeDtypeStruct((query_heads, tokens, size), jnp.bfloat16)
    params = pltpu.CompilerParams(vmem_limit_bytes=VMEM_LIMIT)

    def term(count):
        return jax.ShapeDtypeStruct((count, 2, tokens, size), jnp.bfloat16)

    def square(count, kind=jnp.float32):
        return pltpu.VMEM((2, count, tokens, tokens), kind)

    def local(own):
        n = len(LOCAL)
        return pl.pallas_call(
            functools.partial(local_kernel, scale),
            grid=(heads_all,),
            in_specs=[VMEM, rows(0)] + [block(0, 0)] * n,
            out_specs=[exps(0), rows(0), rows(0)],
            out_shape=[jax.ShapeDtypeStruct((query_heads, n, tokens, tokens), jnp.bfloat16), wide, wide],
            scratch_shapes=[square(n)],
            compiler_params=params,
            cost_estimate=cost(2, heads_all, head_group, tokens, n, size),
        )(bias, in_hbm(queries), *own)

    def remote(heads, part, stat, others, chain):
        first, last = heads
        n = len(REMOTE)
        whole = [rows(first)] * 3 + [block(first, 0)]
        return pl.pallas_call(
            functools.partial(remote_kernel, scale, len(chain)),
            grid=(last - first,),
            in_specs=[VMEM] + [rows(first)] * 4 + [block(first, begin) for _, begin in others] + [ANY] * len(chain),
            out_specs=whole + [block(0, 0)] * (n - 1),
            out_shape=[narrow, wide, wide, term(heads_all)] + [term(last - first)] * (n - 1),
            scratch_shapes=[pltpu.VMEM((n, size, tokens), jnp.float32)] * 2
            + [square(n), square(n, jnp.bfloat16), square(n)],
            input_output_aliases={5 + n + i: i for i in range(len(chain))},
            compiler_params=params,
            cost_estimate=cost(6, last - first, head_group, tokens, n, size),
        )(bias, in_hbm(queries), in_hbm(output_gradient), part, stat, *[a for a, _ in others], *chain)

    def rest(heads, e, part, row, own, chain):
        first, last = heads
        n = len(LOCAL)
        return pl.pallas_call(
            functools.partial(rest_kernel, scale, len(chain)),
            grid=(last - first,),
            in_specs=[rows(first)] * 2
            + [exps(first)]
            + [rows(first)] * 2
            + [block(first, 0)] * n
            + [ANY] * len(chain),
            out_specs=[rows(first)] + [block(0, 0)] * n,
            out_shape=[narrow] + [term(last - first)] * n,
            scratch_shapes=[pltpu.VMEM((n, size, tokens), jnp.float32)] * 2 + [square(n)],
            input_output_aliases={5 + n + i: i for i in range(len(chain))},
            compiler_params=params,
            cost_estimate=cost(4, last - first, head_group, tokens, n, size),
        )(in_hbm(queries), in_hbm(output_gradient), e, part, row, *own, *chain)

    return local, remote, rest


def shards(block_mask, queries, keys, values, output_gradient):
    count = lax.axis_size("seq")
    me = lax.axis_index("seq").astype(jnp.int32).reshape(1)
    tokens, kv_heads, size = keys.shape
    head_group = queries.shape[1] // kv_heads
    bits = partner_bits(count)
    q = jnp.transpose(queries, (1, 0, 2))
    dout = jnp.transpose(output_gradient, (1, 0, 2))
    whole = (0, kv_heads)
    groups = (whole,) + HALVES
    bias, *arrays = pack(me, block_mask, keys, values, groups, bits)
    packed = dict(zip(groups, arrays))
    far = {(heads, bit): from_partner(packed[heads], "seq", bit) for heads in HALVES for bit in reversed(bits[2:])}
    core = from_partner(packed[whole], "seq", bits[0])
    near = from_partner(packed[whole], "seq", bits[1])
    local, remote, rest = attend(bias, q, dout, kv_heads, head_group)
    own = [packed[whole], core]
    e, part, stat = local(own)
    chain, sent, terms, term_groups = [], [], [], []
    for heads in HALVES:
        others = [(near, 0)] + [(far[heads, bit], heads[0]) for bit in bits[2:]]
        results = remote(heads, part, stat, others, chain)
        chain = results[:4]
        back = results[4:]
        for bit, term in reversed(list(zip(bits[2:], back))):
            sent.append(from_partner(term, "seq", bit))
            term_groups.append(heads)
    terms = list(sent)
    attended, grad_part, row, near_term = chain
    terms.append(from_partner(near_term, "seq", bits[1]))
    early = len(bits[2:]) * (len(HALVES) - 1)
    row = lax.optimization_barrier((row, *terms[:early]))[0]
    last_groups, last, chain = [whole], [], []
    for heads in HALVES:
        grad_queries, own_term, core_term = rest(heads, e, grad_part, row, own, chain)
        chain = [grad_queries]
        last += [from_partner(core_term, "seq", bits[0]), own_term]
        last_groups += [heads] * 2
    term_groups.append(whole)
    gathered = gather_terms(term_groups, terms, kv_heads)
    grad_keys, grad_values = sum_terms(last_groups, [gathered] + last, tokens, kv_heads, size)
    return (jnp.transpose(attended, (1, 0, 2)), jnp.transpose(grad_queries, (1, 0, 2)), grad_keys, grad_values)


def solution(mesh):
    rows = P(("groups", "seq"), None)
    cube = P(("groups", "seq"), None, None)
    return jax.shard_map(
        shards,
        mesh=mesh,
        in_specs=(rows, cube, cube, cube, cube),
        out_specs=(cube, cube, cube, cube),
        check_vma=False,
    )
```

```python
import functools

import jax
import jax.numpy as jnp
from jax import lax
from jax.experimental import pallas as pl
from jax.experimental.pallas import tpu as pltpu
from jax.sharding import PartitionSpec as P

LOG2E = 1.4426950408889634
MASKED = -1e30
VMEM_LIMIT = 24 * 2**20
LOCAL = (0, 1)
REMOTE = (2, 3, 4)
HALVES = ((0, 2), (2, 4))


def from_partner(value, axis, apart):
    mask = 2**apart
    pairs = [(source, source ^ mask) for source in range(lax.axis_size(axis))]
    return lax.ppermute(value, axis, pairs)


def partner_bits(count):
    level = count.bit_length() - 1
    return (0, 1, level - 2, level - 1)


def product(left, right):
    return lax.dot_general(left, right, (((1,), (0,)), ((), ())), preferred_element_type=jnp.float32)


def product_nt(left, right):
    return lax.dot_general(left, right, (((1,), (1,)), ((), ())), preferred_element_type=jnp.float32)


VMEM = pl.BlockSpec(memory_space=pltpu.VMEM)
SMEM = pl.BlockSpec(memory_space=pltpu.SMEM)
ANY = pl.BlockSpec(memory_space=pl.ANY)


def in_hbm(array):
    return pltpu.with_memory_space_constraint(array, pltpu.HBM)


def pack_kernel(groups, bits, me_ref, mask_ref, k_ref, v_ref, bias_ref, *refs):
    outs, wide_ref = refs[:-1], refs[-1]
    tokens, heads, size = k_ref.shape
    for i, ref in enumerate((k_ref, v_ref)):
        wide_ref[i] = ref[...].astype(jnp.float32).reshape(tokens * heads, size)
        for h in range(heads):
            rows = wide_ref[i, pl.ds(h, tokens, stride=heads), :].astype(jnp.bfloat16)
            for (low, high), out in zip(groups, outs):
                if low <= h < high:
                    out[h - low, i] = rows
    me = me_ref[0]
    blocks, columns = mask_ref.shape
    mask = mask_ref[...]
    column = lax.broadcasted_iota(jnp.int32, (blocks, columns), 1)
    for s, device in enumerate([me] + [jnp.bitwise_xor(me, 1 << bit) for bit in bits]):
        for b in range(blocks):
            ones = jnp.sum(jnp.where(column == device * blocks + b, mask, 0), axis=1, keepdims=True)
            width = tokens // blocks
            bias_ref[s, :, b * width : (b + 1) * width] = jnp.broadcast_to(
                jnp.where(ones > 0, 0.0, MASKED), (blocks, width)
            )


def pack(me, block_mask, keys, values, groups, bits):
    tokens, heads, size = keys.shape
    bias = jax.ShapeDtypeStruct((len(bits) + 1, block_mask.shape[0], tokens), jnp.float32)
    return pl.pallas_call(
        functools.partial(pack_kernel, groups, bits),
        in_specs=[SMEM] + [VMEM] * 3,
        out_specs=[VMEM] * (len(groups) + 1),
        out_shape=[bias]
        + [jax.ShapeDtypeStruct((high - low, 2, tokens, size), keys.dtype) for low, high in groups],
        scratch_shapes=[pltpu.VMEM((2, tokens * heads, size), jnp.float32)],
        compiler_params=pltpu.CompilerParams(vmem_limit_bytes=VMEM_LIMIT),
        cost_estimate=pl.CostEstimate(flops=0, bytes_accessed=6 * keys.size * 2, transcendentals=0),
    )(me, in_hbm(block_mask), in_hbm(keys), in_hbm(values))


def gather_kernel(groups, *refs):
    terms, out = refs[:-1], refs[-1]
    for h in range(out.shape[0]):
        parts = [t[h - g[0]].astype(jnp.float32) for g, t in zip(groups, terms) if g[0] <= h < g[1]]
        out[h] = functools.reduce(jnp.add, parts)


def gather_terms(groups, terms, heads):
    return pl.pallas_call(
        functools.partial(gather_kernel, groups),
        in_specs=[VMEM] * len(groups),
        out_specs=VMEM,
        out_shape=jax.ShapeDtypeStruct((heads,) + terms[0].shape[1:], jnp.float32),
        compiler_params=pltpu.CompilerParams(vmem_limit_bytes=VMEM_LIMIT),
        cost_estimate=pl.CostEstimate(flops=0, bytes_accessed=8 * 2**20, transcendentals=0),
    )(*terms)


def sum_kernel(groups, *refs):
    terms, (dk_ref, dv_ref, wide_ref) = refs[: len(groups)], refs[len(groups) :]
    tokens, heads, size = dk_ref.shape
    for i, ref in enumerate((dk_ref, dv_ref)):
        for h in range(heads):
            parts = [t[h - g[0], i].astype(jnp.float32) for g, t in zip(groups, terms) if g[0] <= h < g[1]]
            wide_ref[i, pl.ds(h, tokens, stride=heads), :] = functools.reduce(jnp.add, parts)
        ref[...] = wide_ref[i].astype(ref.dtype).reshape(tokens, heads, size)


def sum_terms(groups, terms, tokens, heads, size):
    out = jax.ShapeDtypeStruct((tokens, heads, size), jnp.bfloat16)
    return pl.pallas_call(
        functools.partial(sum_kernel, groups),
        in_specs=[VMEM] * len(groups),
        out_specs=[VMEM] * 2,
        out_shape=[out, out],
        scratch_shapes=[pltpu.VMEM((2, tokens * heads, size), jnp.float32)],
        compiler_params=pltpu.CompilerParams(vmem_limit_bytes=VMEM_LIMIT),
        cost_estimate=pl.CostEstimate(flops=0, bytes_accessed=12 * tokens * heads * size * 2, transcendentals=0),
    )(*terms)


def scores_of(q, key, bias_ref, s):
    x = product_nt(q, key)
    blocks = bias_ref.shape[1]
    width = x.shape[0] // blocks
    return jnp.concatenate([x[a * width : (a + 1) * width] + bias_ref[s, a : a + 1] for a in range(blocks)], axis=0)


def twice(array):
    return jnp.concatenate([array, array], axis=1)


def fill_values(kv_refs, v_ref):
    for n, ref in enumerate(kv_refs):
        value = ref[0, 1]
        v_ref[n] = jnp.concatenate([value, jnp.ones_like(value)], axis=1)


def local_kernel(softmax_scale, bias_ref, q_ref, *refs):
    sources = len(LOCAL)
    kv_refs = refs[:sources]
    e_ref, o_ref, stat_ref, x_ref, v_ref = refs[sources:]
    scale2 = softmax_scale * LOG2E
    head_group, tokens, size = q_ref.shape
    state = {}
    fill_values(kv_refs, v_ref)

    def scores(g, n):
        x = scores_of(q_ref[g], kv_refs[n][0, 0], bias_ref, LOCAL[n])
        x_ref[g % 3, n] = x
        state["max", g] = jnp.maximum(state["max", g], x) if n else x

    def scores_end(g):
        state["top", g] = jnp.max(state.pop(("max", g)), axis=1, keepdims=True) * scale2

    def forward(g, n):
        e = jnp.exp2(x_ref[g % 3, n] * scale2 - state["top", g])
        narrow = e.astype(jnp.bfloat16)
        e_ref[g, n] = narrow
        part = product(narrow, v_ref[n])
        state["out", g] = state["out", g] + part if n else part

    def forward_end(g):
        out = state.pop(("out", g))
        o_ref[g] = out[:, :size]
        stat_ref[g, 0] = jnp.broadcast_to(state["top", g], (tokens, size))
        stat_ref[g, 1] = out[:, size:]

    every = range(sources)
    for g in range(2):
        for n in every:
            scores(g, n)
        scores_end(g)
    for g in range(head_group):
        for n in every:
            forward(g, n)
            if g + 2 < head_group:
                scores(g + 2, n)
        forward_end(g)
        if g + 2 < head_group:
            scores_end(g + 2)


def remote_kernel(softmax_scale, unused, bias_ref, q_ref, do_ref, part_ref, stat_ref, *refs):
    sources = len(REMOTE)
    kv_refs = refs[:sources]
    refs = refs[sources + unused :]
    o_ref, dq_ref, row_ref = refs[:3]
    term_refs = refs[3 : sources + 3]
    dk_ref, dv_ref, x_ref, e_ref, p_ref, v_ref = refs[sources + 3 :]
    scale2 = softmax_scale * LOG2E
    head_group, tokens, size = q_ref.shape
    state = {}
    fill_values(kv_refs, v_ref)

    def key(n):
        return kv_refs[n][0, 0]

    def scores(g, n):
        x = scores_of(q_ref[g], key(n), bias_ref, REMOTE[n])
        x_ref[g % 3, n] = x
        state["max", g] = jnp.maximum(state["max", g], x) if n else x

    def dprob(g, n):
        p_ref[g % 2, n] = product_nt(do_ref[g], kv_refs[n][0, 1])

    def scores_end(g):
        local, total = stat_ref[g, 0], stat_ref[g, 1]
        top = jnp.maximum(jnp.max(state.pop(("max", g)), axis=1, keepdims=True) * scale2, local)
        state["top", g] = top
        state["share", g] = jnp.exp2(local - top)
        state["part", g] = total * state["share", g]

    def forward(g, n):
        e = jnp.exp2(x_ref[g % 3, n] * scale2 - twice(state["top", g]))
        narrow = e.astype(jnp.bfloat16)
        e_ref[g % 2, n] = narrow
        part = product(narrow, v_ref[n])
        state["out", g] = state["out", g] + part if n else part

    def forward_end(g):
        q, do = q_ref[g], do_ref[g].astype(jnp.float32)
        out = state.pop(("out", g))
        share = state.pop(("share", g))
        inverse = 1.0 / (out[:, size:] + state.pop(("part", g)))
        attended = ((out[:, :size] + part_ref[g] * share) * inverse).astype(jnp.bfloat16)
        o_ref[g] = attended
        delta = jnp.sum(do * attended.astype(jnp.float32), axis=1, keepdims=True)
        state["delta", g] = delta
        row_ref[g, 0] = share * inverse
        row_ref[g, 1] = jnp.broadcast_to(delta, (tokens, size))
        state["scale", g] = inverse * softmax_scale
        state["q", g] = (q.astype(jnp.float32) * state["scale", g]).astype(jnp.bfloat16).T
        state["do", g] = (do * inverse).astype(jnp.bfloat16).T

    def backward(g, n):
        e = e_ref[g % 2, n]
        dv = product(state["do", g], e)
        dscore = (e.astype(jnp.float32) * (p_ref[g % 2, n] - state["delta", g])).astype(jnp.bfloat16)
        part = product(dscore, key(n))
        state["dq", g] = state["dq", g] + part if n else part
        dk = product(state["q", g], dscore)
        if g == 0:
            dk_ref[n] = dk
            dv_ref[n] = dv
        elif g < head_group - 1:
            dk_ref[n] += dk
            dv_ref[n] += dv
        else:
            term_refs[n][0, 0] = (dk_ref[n] + dk).T.astype(jnp.bfloat16)
            term_refs[n][0, 1] = (dv_ref[n] + dv).T.astype(jnp.bfloat16)

    def backward_end(g):
        dq_ref[g] = state.pop(("dq", g)) * state["scale", g]

    every = range(sources)
    for g in range(2):
        for n in every:
            scores(g, n)
        scores_end(g)
    for g in range(head_group):
        for n in every:
            forward(g, n)
            if g + 2 < head_group:
                scores(g + 2, n)
            dprob(g, n)
        forward_end(g)
        if g + 2 < head_group:
            scores_end(g + 2)
        if g:
            for n in every:
                backward(g - 1, n)
            backward_end(g - 1)
    for n in every:
        backward(head_group - 1, n)
    backward_end(head_group - 1)


def rest_kernel(softmax_scale, unused, q_ref, do_ref, e_ref, part_ref, row_ref, *refs):
    sources = len(LOCAL)
    kv_refs = refs[:sources]
    refs = refs[sources + unused :]
    dq_ref = refs[0]
    term_refs = refs[1 : sources + 1]
    dk_ref, dv_ref, p_ref = refs[sources + 1 :]
    head_group = q_ref.shape[0]
    state = {}

    def dprob(g, n):
        p_ref[g % 2, n] = product_nt(do_ref[g], kv_refs[n][0, 1])

    def rows(g):
        share = row_ref[g, 0]
        state["delta", g] = twice(row_ref[g, 1])
        state["scale", g] = share * softmax_scale
        state["q", g] = (q_ref[g].astype(jnp.float32) * state["scale", g]).astype(jnp.bfloat16).T
        state["do", g] = (do_ref[g].astype(jnp.float32) * share).astype(jnp.bfloat16).T

    def backward(g, n):
        e = e_ref[g, n]
        dv = product(state["do", g], e)
        dscore = (e.astype(jnp.float32) * (p_ref[g % 2, n] - state["delta", g])).astype(jnp.bfloat16)
        part = product(dscore, kv_refs[n][0, 0])
        state["dq", g] = state["dq", g] + part if n else part
        dk = product(state["q", g], dscore)
        if g == 0:
            dk_ref[n] = dk
            dv_ref[n] = dv
        elif g < head_group - 1:
            dk_ref[n] += dk
            dv_ref[n] += dv
        else:
            term_refs[n][0, 0] = (dk_ref[n] + dk).T.astype(jnp.bfloat16)
            term_refs[n][0, 1] = (dv_ref[n] + dv).T.astype(jnp.bfloat16)

    every = range(sources)
    for n in every:
        dprob(0, n)
    rows(0)
    for g in range(head_group):
        if g + 1 < head_group:
            rows(g + 1)
        for n in every:
            backward(g, n)
            if g + 1 < head_group:
                dprob(g + 1, n)
        dq_ref[g] = (part_ref[g] + state.pop(("dq", g)) * state["scale", g]).astype(jnp.bfloat16)


def cost(products, heads, head_group, tokens, sources, size):
    scores = heads * head_group * tokens * tokens * sources
    return pl.CostEstimate(
        flops=2 * products * scores * size,
        bytes_accessed=8 * heads * head_group * tokens * size,
        transcendentals=scores,
    )


def attend(bias, queries, output_gradient, heads_all, head_group):
    tokens, size = queries.shape[1:]

    def rows(first):
        return pl.BlockSpec((head_group, tokens, size), lambda j: (first + j, 0, 0))

    def block(first, begin):
        return pl.BlockSpec((1, 2, tokens, size), lambda j: (first - begin + j, 0, 0, 0))

    def exps(first):
        return pl.BlockSpec((head_group, len(LOCAL), tokens, tokens), lambda j: (first + j, 0, 0, 0))

    def columns(first):
        return pl.BlockSpec((head_group, 2, tokens, size), lambda j: (first + j, 0, 0, 0))

    scale = size ** (-0.5)
    query_heads = heads_all * head_group
    wide = jax.ShapeDtypeStruct((query_heads, tokens, size), jnp.float32)
    double = jax.ShapeDtypeStruct((query_heads, 2, tokens, size), jnp.float32)
    narrow = jax.ShapeDtypeStruct((query_heads, tokens, size), jnp.bfloat16)
    params = pltpu.CompilerParams(vmem_limit_bytes=VMEM_LIMIT)

    def term(count):
        return jax.ShapeDtypeStruct((count, 2, tokens, size), jnp.bfloat16)

    def square(depth, count, kind=jnp.float32):
        return pltpu.VMEM((depth, count, tokens, tokens), kind)

    def local(own):
        n = len(LOCAL)
        return pl.pallas_call(
            functools.partial(local_kernel, scale),
            grid=(heads_all,),
            in_specs=[VMEM, rows(0)] + [block(0, 0)] * n,
            out_specs=[exps(0), rows(0), columns(0)],
            out_shape=[jax.ShapeDtypeStruct((query_heads, n, tokens, tokens), jnp.bfloat16), wide, double],
            scratch_shapes=[square(3, n), pltpu.VMEM((n, tokens, 2 * size), jnp.bfloat16)],
            compiler_params=params,
            cost_estimate=cost(2, heads_all, head_group, tokens, n, size),
        )(bias, in_hbm(queries), *own)

    def remote(heads, part, stat, others, chain):
        first, last = heads
        n = len(REMOTE)
        whole = [rows(first)] * 2 + [columns(first), block(first, 0)]
        return pl.pallas_call(
            functools.partial(remote_kernel, scale, len(chain)),
            grid=(last - first,),
            in_specs=[VMEM] + [rows(first)] * 3 + [columns(first)] + [block(first, begin) for _, begin in others] + [ANY] * len(chain),
            out_specs=whole + [block(0, 0)] * (n - 1),
            out_shape=[narrow, wide, double, term(heads_all)] + [term(last - first)] * (n - 1),
            scratch_shapes=[pltpu.VMEM((n, size, tokens), jnp.float32)] * 2
            + [square(3, n), square(2, n, jnp.bfloat16), square(2, n), pltpu.VMEM((n, tokens, 2 * size), jnp.bfloat16)],
            input_output_aliases={5 + n + i: i for i in range(len(chain))},
            compiler_params=params,
            cost_estimate=cost(6, last - first, head_group, tokens, n, size),
        )(bias, in_hbm(queries), in_hbm(output_gradient), part, stat, *[a for a, _ in others], *chain)

    def rest(heads, e, part, row, own, chain):
        first, last = heads
        n = len(LOCAL)
        return pl.pallas_call(
            functools.partial(rest_kernel, scale, len(chain)),
            grid=(last - first,),
            in_specs=[rows(first)] * 2
            + [exps(first)]
            + [rows(first), columns(first)]
            + [block(first, 0)] * n
            + [ANY] * len(chain),
            out_specs=[rows(first)] + [block(0, 0)] * n,
            out_shape=[narrow] + [term(last - first)] * n,
            scratch_shapes=[pltpu.VMEM((n, size, tokens), jnp.float32)] * 2 + [square(2, n)],
            input_output_aliases={5 + n + i: i for i in range(len(chain))},
            compiler_params=params,
            cost_estimate=cost(4, last - first, head_group, tokens, n, size),
        )(in_hbm(queries), in_hbm(output_gradient), e, part, row, *own, *chain)

    return local, remote, rest


def shards(block_mask, queries, keys, values, output_gradient):
    count = lax.axis_size("seq")
    me = lax.axis_index("seq").astype(jnp.int32).reshape(1)
    tokens, kv_heads, size = keys.shape
    head_group = queries.shape[1] // kv_heads
    bits = partner_bits(count)
    q = jnp.transpose(queries, (1, 0, 2))
    dout = jnp.transpose(output_gradient, (1, 0, 2))
    whole = (0, kv_heads)
    groups = (whole,) + HALVES
    bias, *arrays = pack(me, block_mask, keys, values, groups, bits)
    packed = dict(zip(groups, arrays))
    far = {(HALVES[0], bit): from_partner(packed[HALVES[0]], "seq", bit) for bit in reversed(bits[2:])}
    core = from_partner(packed[whole], "seq", bits[0])
    near = {HALVES[0]: from_partner(packed[HALVES[0]], "seq", bits[1])}
    local, remote, rest = attend(bias, q, dout, kv_heads, head_group)
    own = [packed[whole], core]
    e, part, stat = local(own)
    for heads in HALVES[1:]:
        later = lax.optimization_barrier((packed[heads], stat))[0]
        far.update({(heads, bit): from_partner(later, "seq", bit) for bit in reversed(bits[2:])})
        near[heads] = from_partner(later, "seq", bits[1])
    chain, sent, terms, term_groups = [], [], [], []
    for heads in HALVES:
        others = [(near[heads], heads[0])] + [(far[heads, bit], heads[0]) for bit in bits[2:]]
        results = remote(heads, part, stat, others, chain)
        chain = results[:4]
        back = results[4:]
        for bit, term in reversed(list(zip(bits[2:], back))):
            sent.append(from_partner(term, "seq", bit))
            term_groups.append(heads)
    terms = list(sent)
    attended, grad_part, row, near_term = chain
    terms.append(from_partner(near_term, "seq", bits[1]))
    early = len(bits[2:]) * (len(HALVES) - 1)
    row = lax.optimization_barrier((row, *terms[:early]))[0]
    last_groups, last, chain = [whole], [], []
    for heads in HALVES:
        grad_queries, own_term, core_term = rest(heads, e, grad_part, row, own, chain)
        chain = [grad_queries]
        last += [from_partner(core_term, "seq", bits[0]), own_term]
        last_groups += [heads] * 2
    term_groups.append(whole)
    gathered = gather_terms(term_groups, terms, kv_heads)
    grad_keys, grad_values = sum_terms(last_groups, [gathered] + last, tokens, kv_heads, size)
    return (jnp.transpose(attended, (1, 0, 2)), jnp.transpose(grad_queries, (1, 0, 2)), grad_keys, grad_values)


def solution(mesh):
    rows = P(("groups", "seq"), None)
    cube = P(("groups", "seq"), None, None)
    return jax.shard_map(
        shards,
        mesh=mesh,
        in_specs=(rows, cube, cube, cube, cube),
        out_specs=(cube, cube, cube, cube),
        check_vma=False,
    )
```

```python
import functools

import jax
import jax.numpy as jnp
from jax import lax
from jax.experimental import pallas as pl
from jax.experimental.pallas import tpu as pltpu
from jax.sharding import PartitionSpec as P

LOG2E = 1.4426950408889634
MASKED = -1e30
VMEM_LIMIT = 24 * 2**20
PAD = 32
LOCAL = (0, 1)
REMOTE = (2, 3, 4)
HALVES = ((0, 2), (2, 4))


def from_partner(value, axis, apart):
    mask = 2**apart
    pairs = [(source, source ^ mask) for source in range(lax.axis_size(axis))]
    return lax.ppermute(value, axis, pairs)


def partner_bits(count):
    level = count.bit_length() - 1
    return (0, 1, level - 2, level - 1)


def product(left, right):
    return lax.dot_general(left, right, (((1,), (0,)), ((), ())), preferred_element_type=jnp.float32)


def product_nt(left, right):
    return lax.dot_general(left, right, (((1,), (1,)), ((), ())), preferred_element_type=jnp.float32)


VMEM = pl.BlockSpec(memory_space=pltpu.VMEM)
SMEM = pl.BlockSpec(memory_space=pltpu.SMEM)
ANY = pl.BlockSpec(memory_space=pl.ANY)


def in_hbm(array):
    return pltpu.with_memory_space_constraint(array, pltpu.HBM)


def pack_kernel(groups, k_ref, v_ref, *refs):
    outs, wide_ref = refs[:-1], refs[-1]
    tokens, heads, size = k_ref.shape
    for i, ref in enumerate((k_ref, v_ref)):
        wide_ref[i, : tokens * heads] = ref[...].astype(jnp.float32).reshape(tokens * heads, size)
        for h in range(heads):
            rows = wide_ref[i, pl.ds(h, tokens, stride=heads), :].astype(jnp.bfloat16)
            for (low, high), out in zip(groups, outs):
                if low <= h < high:
                    out[h - low, i] = rows


def pack(keys, values, groups):
    tokens, heads, size = keys.shape
    return pl.pallas_call(
        functools.partial(pack_kernel, groups),
        in_specs=[VMEM] * 2,
        out_specs=[VMEM] * len(groups),
        out_shape=[jax.ShapeDtypeStruct((high - low, 2, tokens, size), keys.dtype) for low, high in groups],
        scratch_shapes=[pltpu.VMEM((2, tokens * heads + PAD, size), jnp.float32)],
        compiler_params=pltpu.CompilerParams(vmem_limit_bytes=VMEM_LIMIT),
        cost_estimate=pl.CostEstimate(flops=0, bytes_accessed=6 * keys.size * 2, transcendentals=0),
    )(in_hbm(keys), in_hbm(values))


def mask_kernel(bits, me_ref, mask_ref, bias_ref):
    me = me_ref[0]
    blocks, columns = mask_ref.shape
    width = bias_ref.shape[2] // blocks
    mask = mask_ref[...]
    column = lax.broadcasted_iota(jnp.int32, (blocks, columns), 1)
    for s, device in enumerate([me] + [jnp.bitwise_xor(me, 1 << bit) for bit in bits]):
        for b in range(blocks):
            ones = jnp.sum(jnp.where(column == device * blocks + b, mask, 0), axis=1, keepdims=True)
            bias_ref[s, :, b * width : (b + 1) * width] = jnp.broadcast_to(
                jnp.where(ones > 0, 0.0, MASKED), (blocks, width)
            )


def mask_rows(me, block_mask, tokens, bits):
    return pl.pallas_call(
        functools.partial(mask_kernel, bits),
        in_specs=[SMEM, VMEM],
        out_specs=VMEM,
        out_shape=jax.ShapeDtypeStruct((len(bits) + 1, block_mask.shape[0], tokens), jnp.float32),
        compiler_params=pltpu.CompilerParams(vmem_limit_bytes=VMEM_LIMIT),
        cost_estimate=pl.CostEstimate(flops=0, bytes_accessed=2**14, transcendentals=0),
    )(me, in_hbm(block_mask))


def gather_kernel(groups, *refs):
    terms, out = refs[:-1], refs[-1]
    for h in range(out.shape[0]):
        parts = [t[h - g[0]].astype(jnp.float32) for g, t in zip(groups, terms) if g[0] <= h < g[1]]
        out[h] = functools.reduce(jnp.add, parts)


def gather_terms(groups, terms, heads):
    return pl.pallas_call(
        functools.partial(gather_kernel, groups),
        in_specs=[VMEM] * len(groups),
        out_specs=VMEM,
        out_shape=jax.ShapeDtypeStruct((heads,) + terms[0].shape[1:], jnp.float32),
        compiler_params=pltpu.CompilerParams(vmem_limit_bytes=VMEM_LIMIT),
        cost_estimate=pl.CostEstimate(flops=0, bytes_accessed=8 * 2**20, transcendentals=0),
    )(*terms)


def sum_kernel(groups, *refs):
    terms, (dk_ref, dv_ref, wide_ref) = refs[: len(groups)], refs[len(groups) :]
    tokens, heads, size = dk_ref.shape
    for i, ref in enumerate((dk_ref, dv_ref)):
        for h in range(heads):
            parts = [t[h - g[0], i].astype(jnp.float32) for g, t in zip(groups, terms) if g[0] <= h < g[1]]
            wide_ref[i, pl.ds(h, tokens, stride=heads), :] = functools.reduce(jnp.add, parts)
        ref[...] = wide_ref[i, : tokens * heads].astype(ref.dtype).reshape(tokens, heads, size)


def sum_terms(groups, terms, tokens, heads, size):
    out = jax.ShapeDtypeStruct((tokens, heads, size), jnp.bfloat16)
    return pl.pallas_call(
        functools.partial(sum_kernel, groups),
        in_specs=[VMEM] * len(groups),
        out_specs=[VMEM] * 2,
        out_shape=[out, out],
        scratch_shapes=[pltpu.VMEM((2, tokens * heads + PAD, size), jnp.float32)],
        compiler_params=pltpu.CompilerParams(vmem_limit_bytes=VMEM_LIMIT),
        cost_estimate=pl.CostEstimate(flops=0, bytes_accessed=12 * tokens * heads * size * 2, transcendentals=0),
    )(*terms)


def scores_of(q, key, bias_ref, s):
    x = product_nt(q, key)
    blocks = bias_ref.shape[1]
    width = x.shape[0] // blocks
    return jnp.concatenate([x[a * width : (a + 1) * width] + bias_ref[s, a : a + 1] for a in range(blocks)], axis=0)


def twice(array):
    return jnp.concatenate([array, array], axis=1)


def fill_values(kv_refs, v_ref):
    for n, ref in enumerate(kv_refs):
        value = ref[0, 1]
        v_ref[n] = jnp.concatenate([value, jnp.ones_like(value)], axis=1)


def local_kernel(softmax_scale, bias_ref, q_ref, *refs):
    sources = len(LOCAL)
    kv_refs = refs[:sources]
    e_ref, o_ref, stat_ref, x_ref, v_ref = refs[sources:]
    scale2 = softmax_scale * LOG2E
    head_group, tokens, size = q_ref.shape
    state = {}
    fill_values(kv_refs, v_ref)

    def scores(g, n):
        x = scores_of(q_ref[g], kv_refs[n][0, 0], bias_ref, LOCAL[n])
        x_ref[g % 3, n] = x
        state["max", g] = jnp.maximum(state["max", g], x) if n else x

    def scores_end(g):
        state["top", g] = jnp.max(state.pop(("max", g)), axis=1, keepdims=True) * scale2

    def forward(g, n):
        e = jnp.exp2(x_ref[g % 3, n] * scale2 - state["top", g])
        narrow = e.astype(jnp.bfloat16)
        e_ref[g, n] = narrow
        part = product(narrow, v_ref[n])
        state["out", g] = state["out", g] + part if n else part

    def forward_end(g):
        out = state.pop(("out", g))
        o_ref[g] = out[:, :size]
        stat_ref[g, 0] = jnp.broadcast_to(state["top", g], (tokens, size))
        stat_ref[g, 1] = out[:, size:]

    every = range(sources)
    for g in range(2):
        for n in every:
            scores(g, n)
        scores_end(g)
    for g in range(head_group):
        for n in every:
            forward(g, n)
            if g + 2 < head_group:
                scores(g + 2, n)
        forward_end(g)
        if g + 2 < head_group:
            scores_end(g + 2)


def remote_kernel(softmax_scale, unused, bias_ref, q_ref, do_ref, part_ref, stat_ref, *refs):
    sources = len(REMOTE)
    kv_refs = refs[:sources]
    refs = refs[sources + unused :]
    o_ref, dq_ref, row_ref = refs[:3]
    term_refs = refs[3 : sources + 3]
    dk_ref, dv_ref, x_ref, e_ref, p_ref, v_ref = refs[sources + 3 :]
    scale2 = softmax_scale * LOG2E
    head_group, tokens, size = q_ref.shape
    state = {}
    fill_values(kv_refs, v_ref)

    def key(n):
        return kv_refs[n][0, 0]

    def scores(g, n):
        x = scores_of(q_ref[g], key(n), bias_ref, REMOTE[n])
        x_ref[g % 3, n] = x
        state["max", g] = jnp.maximum(state["max", g], x) if n else x

    def dprob(g, n):
        p_ref[g % 2, n] = product_nt(do_ref[g], kv_refs[n][0, 1])

    def scores_end(g):
        local, total = stat_ref[g, 0], stat_ref[g, 1]
        top = jnp.maximum(jnp.max(state.pop(("max", g)), axis=1, keepdims=True) * scale2, local)
        state["top", g] = top
        state["share", g] = jnp.exp2(local - top)
        state["part", g] = total * state["share", g]

    def forward(g, n):
        e = jnp.exp2(x_ref[g % 3, n] * scale2 - twice(state["top", g]))
        narrow = e.astype(jnp.bfloat16)
        e_ref[g % 2, n] = narrow
        part = product(narrow, v_ref[n])
        state["out", g] = state["out", g] + part if n else part

    def forward_end(g):
        q, do = q_ref[g], do_ref[g].astype(jnp.float32)
        out = state.pop(("out", g))
        share = state.pop(("share", g))
        inverse = 1.0 / (out[:, size:] + state.pop(("part", g)))
        attended = ((out[:, :size] + part_ref[g] * share) * inverse).astype(jnp.bfloat16)
        o_ref[g] = attended
        delta = jnp.sum(do * attended.astype(jnp.float32), axis=1, keepdims=True)
        state["delta", g] = delta
        row_ref[g, 0] = share * inverse
        row_ref[g, 1] = jnp.broadcast_to(delta, (tokens, size))
        state["scale", g] = inverse * softmax_scale
        state["q", g] = (q.astype(jnp.float32) * state["scale", g]).astype(jnp.bfloat16).T
        state["do", g] = (do * inverse).astype(jnp.bfloat16).T

    def backward(g, n):
        e = e_ref[g % 2, n]
        dv = product(state["do", g], e)
        dscore = (e.astype(jnp.float32) * (p_ref[g % 2, n] - state["delta", g])).astype(jnp.bfloat16)
        part = product(dscore, key(n))
        state["dq", g] = state["dq", g] + part if n else part
        dk = product(state["q", g], dscore)
        if g == 0:
            dk_ref[n] = dk
            dv_ref[n] = dv
        elif g < head_group - 1:
            dk_ref[n] += dk
            dv_ref[n] += dv
        else:
            term_refs[n][0, 0] = (dk_ref[n] + dk).T.astype(jnp.bfloat16)
            term_refs[n][0, 1] = (dv_ref[n] + dv).T.astype(jnp.bfloat16)

    def backward_end(g):
        dq_ref[g] = state.pop(("dq", g)) * state["scale", g]

    every = range(sources)
    for g in range(2):
        for n in every:
            scores(g, n)
        scores_end(g)
    for g in range(head_group):
        for n in every:
            forward(g, n)
            if g + 2 < head_group:
                scores(g + 2, n)
            dprob(g, n)
        forward_end(g)
        if g + 2 < head_group:
            scores_end(g + 2)
        if g:
            for n in every:
                backward(g - 1, n)
            backward_end(g - 1)
    for n in every:
        backward(head_group - 1, n)
    backward_end(head_group - 1)


def rest_kernel(softmax_scale, unused, q_ref, do_ref, e_ref, part_ref, row_ref, *refs):
    sources = len(LOCAL)
    kv_refs = refs[:sources]
    refs = refs[sources + unused :]
    dq_ref = refs[0]
    term_refs = refs[1 : sources + 1]
    dk_ref, dv_ref, p_ref = refs[sources + 1 :]
    head_group = q_ref.shape[0]
    state = {}

    def dprob(g, n):
        p_ref[g % 2, n] = product_nt(do_ref[g], kv_refs[n][0, 1])

    def rows(g):
        share = row_ref[g, 0]
        state["delta", g] = twice(row_ref[g, 1])
        state["scale", g] = share * softmax_scale
        state["q", g] = (q_ref[g].astype(jnp.float32) * state["scale", g]).astype(jnp.bfloat16).T
        state["do", g] = (do_ref[g].astype(jnp.float32) * share).astype(jnp.bfloat16).T

    def backward(g, n):
        e = e_ref[g, n]
        dv = product(state["do", g], e)
        dscore = (e.astype(jnp.float32) * (p_ref[g % 2, n] - state["delta", g])).astype(jnp.bfloat16)
        part = product(dscore, kv_refs[n][0, 0])
        state["dq", g] = state["dq", g] + part if n else part
        dk = product(state["q", g], dscore)
        if g == 0:
            dk_ref[n] = dk
            dv_ref[n] = dv
        elif g < head_group - 1:
            dk_ref[n] += dk
            dv_ref[n] += dv
        else:
            term_refs[n][0, 0] = (dk_ref[n] + dk).T.astype(jnp.bfloat16)
            term_refs[n][0, 1] = (dv_ref[n] + dv).T.astype(jnp.bfloat16)

    every = range(sources)
    for n in every:
        dprob(0, n)
    rows(0)
    for g in range(head_group):
        if g + 1 < head_group:
            rows(g + 1)
        for n in every:
            backward(g, n)
            if g + 1 < head_group:
                dprob(g + 1, n)
        dq_ref[g] = (part_ref[g] + state.pop(("dq", g)) * state["scale", g]).astype(jnp.bfloat16)


def cost(products, heads, head_group, tokens, sources, size):
    scores = heads * head_group * tokens * tokens * sources
    return pl.CostEstimate(
        flops=2 * products * scores * size,
        bytes_accessed=8 * heads * head_group * tokens * size,
        transcendentals=scores,
    )


def attend(bias, queries, output_gradient, heads_all, head_group):
    tokens, size = queries.shape[1:]

    def rows(first):
        return pl.BlockSpec((head_group, tokens, size), lambda j: (first + j, 0, 0))

    def block(first, begin):
        return pl.BlockSpec((1, 2, tokens, size), lambda j: (first - begin + j, 0, 0, 0))

    def exps(first):
        return pl.BlockSpec((head_group, len(LOCAL), tokens, tokens), lambda j: (first + j, 0, 0, 0))

    def columns(first):
        return pl.BlockSpec((head_group, 2, tokens, size), lambda j: (first + j, 0, 0, 0))

    scale = size ** (-0.5)
    query_heads = heads_all * head_group
    wide = jax.ShapeDtypeStruct((query_heads, tokens, size), jnp.float32)
    double = jax.ShapeDtypeStruct((query_heads, 2, tokens, size), jnp.float32)
    narrow = jax.ShapeDtypeStruct((query_heads, tokens, size), jnp.bfloat16)
    params = pltpu.CompilerParams(vmem_limit_bytes=VMEM_LIMIT)

    def term(count):
        return jax.ShapeDtypeStruct((count, 2, tokens, size), jnp.bfloat16)

    def square(depth, count, kind=jnp.float32):
        return pltpu.VMEM((depth, count, tokens, tokens), kind)

    def local(own):
        n = len(LOCAL)
        return pl.pallas_call(
            functools.partial(local_kernel, scale),
            grid=(heads_all,),
            in_specs=[VMEM, rows(0)] + [block(0, 0)] * n,
            out_specs=[exps(0), rows(0), columns(0)],
            out_shape=[jax.ShapeDtypeStruct((query_heads, n, tokens, tokens), jnp.bfloat16), wide, double],
            scratch_shapes=[square(3, n), pltpu.VMEM((n, tokens, 2 * size), jnp.bfloat16)],
            compiler_params=params,
            cost_estimate=cost(2, heads_all, head_group, tokens, n, size),
        )(bias, in_hbm(queries), *own)

    def remote(heads, part, stat, others, chain):
        first, last = heads
        n = len(REMOTE)
        whole = [rows(first)] * 2 + [columns(first), block(first, 0)]
        return pl.pallas_call(
            functools.partial(remote_kernel, scale, len(chain)),
            grid=(last - first,),
            in_specs=[VMEM] + [rows(first)] * 3 + [columns(first)] + [block(first, begin) for _, begin in others] + [ANY] * len(chain),
            out_specs=whole + [block(0, 0)] * (n - 1),
            out_shape=[narrow, wide, double, term(heads_all)] + [term(last - first)] * (n - 1),
            scratch_shapes=[pltpu.VMEM((n, size, tokens), jnp.float32)] * 2
            + [square(3, n), square(2, n, jnp.bfloat16), square(2, n), pltpu.VMEM((n, tokens, 2 * size), jnp.bfloat16)],
            input_output_aliases={5 + n + i: i for i in range(len(chain))},
            compiler_params=params,
            cost_estimate=cost(6, last - first, head_group, tokens, n, size),
        )(bias, in_hbm(queries), in_hbm(output_gradient), part, stat, *[a for a, _ in others], *chain)

    def rest(heads, e, part, row, own, chain):
        first, last = heads
        n = len(LOCAL)
        return pl.pallas_call(
            functools.partial(rest_kernel, scale, len(chain)),
            grid=(last - first,),
            in_specs=[rows(first)] * 2
            + [exps(first)]
            + [rows(first), columns(first)]
            + [block(first, 0)] * n
            + [ANY] * len(chain),
            out_specs=[rows(first)] + [block(0, 0)] * n,
            out_shape=[narrow] + [term(last - first)] * n,
            scratch_shapes=[pltpu.VMEM((n, size, tokens), jnp.float32)] * 2 + [square(2, n)],
            input_output_aliases={5 + n + i: i for i in range(len(chain))},
            compiler_params=params,
            cost_estimate=cost(4, last - first, head_group, tokens, n, size),
        )(in_hbm(queries), in_hbm(output_gradient), e, part, row, *own, *chain)

    return local, remote, rest


def shards(block_mask, queries, keys, values, output_gradient):
    count = lax.axis_size("seq")
    me = lax.axis_index("seq").astype(jnp.int32).reshape(1)
    tokens, kv_heads, size = keys.shape
    head_group = queries.shape[1] // kv_heads
    bits = partner_bits(count)
    q = jnp.transpose(queries, (1, 0, 2))
    dout = jnp.transpose(output_gradient, (1, 0, 2))
    whole = (0, kv_heads)
    groups = (whole,) + HALVES
    packed = dict(zip(groups, pack(keys, values, groups)))
    bias = mask_rows(me, block_mask, tokens, bits)
    far = {(HALVES[0], bit): from_partner(packed[HALVES[0]], "seq", bit) for bit in reversed(bits[2:])}
    core = from_partner(packed[whole], "seq", bits[0])
    near = {HALVES[0]: from_partner(packed[HALVES[0]], "seq", bits[1])}
    local, remote, rest = attend(bias, q, dout, kv_heads, head_group)
    own = [packed[whole], core]
    e, part, stat = local(own)
    for heads in HALVES[1:]:
        later = lax.optimization_barrier((packed[heads], stat))[0]
        far.update({(heads, bit): from_partner(later, "seq", bit) for bit in reversed(bits[2:])})
        near[heads] = from_partner(later, "seq", bits[1])
    chain, sent, terms, term_groups = [], [], [], []
    for heads in HALVES:
        others = [(near[heads], heads[0])] + [(far[heads, bit], heads[0]) for bit in bits[2:]]
        results = remote(heads, part, stat, others, chain)
        chain = results[:4]
        back = results[4:]
        for bit, term in reversed(list(zip(bits[2:], back))):
            sent.append(from_partner(term, "seq", bit))
            term_groups.append(heads)
    terms = list(sent)
    attended, grad_part, row, near_term = chain
    terms.append(from_partner(near_term, "seq", bits[1]))
    early = len(bits[2:]) * (len(HALVES) - 1)
    row = lax.optimization_barrier((row, *terms[:early]))[0]
    last_groups, last, chain = [whole], [], []
    for heads in HALVES:
        grad_queries, own_term, core_term = rest(heads, e, grad_part, row, own, chain)
        chain = [grad_queries]
        last += [from_partner(core_term, "seq", bits[0]), own_term]
        last_groups += [heads] * 2
    term_groups.append(whole)
    gathered = gather_terms(term_groups, terms, kv_heads)
    grad_keys, grad_values = sum_terms(last_groups, [gathered] + last, tokens, kv_heads, size)
    return (jnp.transpose(attended, (1, 0, 2)), jnp.transpose(grad_queries, (1, 0, 2)), grad_keys, grad_values)


def solution(mesh):
    rows = P(("groups", "seq"), None)
    cube = P(("groups", "seq"), None, None)
    return jax.shard_map(
        shards,
        mesh=mesh,
        in_specs=(rows, cube, cube, cube, cube),
        out_specs=(cube, cube, cube, cube),
        check_vma=False,
    )
```

```python
import functools

import jax
import jax.numpy as jnp
from jax import lax
from jax.experimental import pallas as pl
from jax.experimental.pallas import tpu as pltpu
from jax.sharding import PartitionSpec as P

LOG2E = 1.4426950408889634
MASKED = -1e30
VMEM_LIMIT = 24 * 2**20
PAD = 32
LOCAL = (0, 1)
REMOTE = (2, 3, 4)
HALVES = ((0, 2), (2, 4))


def from_partner(value, axis, apart):
    mask = 2**apart
    pairs = [(source, source ^ mask) for source in range(lax.axis_size(axis))]
    return lax.ppermute(value, axis, pairs)


def partner_bits(count):
    level = count.bit_length() - 1
    return (0, 1, level - 2, level - 1)


def product(left, right):
    return lax.dot_general(left, right, (((1,), (0,)), ((), ())), preferred_element_type=jnp.float32)


def product_nt(left, right):
    return lax.dot_general(left, right, (((1,), (1,)), ((), ())), preferred_element_type=jnp.float32)


VMEM = pl.BlockSpec(memory_space=pltpu.VMEM)
SMEM = pl.BlockSpec(memory_space=pltpu.SMEM)
ANY = pl.BlockSpec(memory_space=pl.ANY)


def in_hbm(array):
    return pltpu.with_memory_space_constraint(array, pltpu.HBM)


def pack_kernel(groups, k_ref, v_ref, *refs):
    outs, wide_ref = refs[:-1], refs[-1]
    tokens, heads, size = k_ref.shape
    for i, ref in enumerate((k_ref, v_ref)):
        wide_ref[i, : tokens * heads] = ref[...].astype(jnp.float32).reshape(tokens * heads, size)
        for h in range(heads):
            rows = wide_ref[i, pl.ds(h, tokens, stride=heads), :].astype(jnp.bfloat16)
            for (low, high), out in zip(groups, outs):
                if low <= h < high:
                    out[h - low, i] = rows


def pack(keys, values, groups):
    tokens, heads, size = keys.shape
    return pl.pallas_call(
        functools.partial(pack_kernel, groups),
        in_specs=[VMEM] * 2,
        out_specs=[VMEM] * len(groups),
        out_shape=[jax.ShapeDtypeStruct((high - low, 2, tokens, size), keys.dtype) for low, high in groups],
        scratch_shapes=[pltpu.VMEM((2, tokens * heads + PAD, size), jnp.float32)],
        compiler_params=pltpu.CompilerParams(vmem_limit_bytes=VMEM_LIMIT),
        cost_estimate=pl.CostEstimate(flops=0, bytes_accessed=6 * keys.size * 2, transcendentals=0),
    )(in_hbm(keys), in_hbm(values))


def mask_kernel(bits, me_ref, mask_ref, bias_ref):
    me = me_ref[0]
    blocks, columns = mask_ref.shape
    width = bias_ref.shape[2] // blocks
    mask = mask_ref[...]
    column = lax.broadcasted_iota(jnp.int32, (blocks, columns), 1)
    for s, device in enumerate([me] + [jnp.bitwise_xor(me, 1 << bit) for bit in bits]):
        for b in range(blocks):
            ones = jnp.sum(jnp.where(column == device * blocks + b, mask, 0), axis=1, keepdims=True)
            bias_ref[s, :, b * width : (b + 1) * width] = jnp.broadcast_to(
                jnp.where(ones > 0, 0.0, MASKED), (blocks, width)
            )


def mask_rows(me, block_mask, tokens, bits):
    return pl.pallas_call(
        functools.partial(mask_kernel, bits),
        in_specs=[SMEM, VMEM],
        out_specs=VMEM,
        out_shape=jax.ShapeDtypeStruct((len(bits) + 1, block_mask.shape[0], tokens), jnp.float32),
        compiler_params=pltpu.CompilerParams(vmem_limit_bytes=VMEM_LIMIT),
        cost_estimate=pl.CostEstimate(flops=0, bytes_accessed=2**14, transcendentals=0),
    )(me, in_hbm(block_mask))


def gather_kernel(groups, *refs):
    terms, out = refs[:-1], refs[-1]
    for h in range(out.shape[0]):
        parts = [t[h - g[0]].astype(jnp.float32) for g, t in zip(groups, terms) if g[0] <= h < g[1]]
        out[h] = functools.reduce(jnp.add, parts)


def gather_terms(groups, terms, heads):
    return pl.pallas_call(
        functools.partial(gather_kernel, groups),
        in_specs=[VMEM] * len(groups),
        out_specs=VMEM,
        out_shape=jax.ShapeDtypeStruct((heads,) + terms[0].shape[1:], jnp.float32),
        compiler_params=pltpu.CompilerParams(vmem_limit_bytes=VMEM_LIMIT),
        cost_estimate=pl.CostEstimate(flops=0, bytes_accessed=8 * 2**20, transcendentals=0),
    )(*terms)


def sum_kernel(groups, *refs):
    terms, (dk_ref, dv_ref, wide_ref) = refs[: len(groups)], refs[len(groups) :]
    tokens, heads, size = dk_ref.shape
    for i, ref in enumerate((dk_ref, dv_ref)):
        for h in range(heads):
            parts = [t[h - g[0], i].astype(jnp.float32) for g, t in zip(groups, terms) if g[0] <= h < g[1]]
            wide_ref[i, pl.ds(h, tokens, stride=heads), :] = functools.reduce(jnp.add, parts)
        ref[...] = wide_ref[i, : tokens * heads].astype(ref.dtype).reshape(tokens, heads, size)


def sum_terms(groups, terms, tokens, heads, size):
    out = jax.ShapeDtypeStruct((tokens, heads, size), jnp.bfloat16)
    return pl.pallas_call(
        functools.partial(sum_kernel, groups),
        in_specs=[VMEM] * len(groups),
        out_specs=[VMEM] * 2,
        out_shape=[out, out],
        scratch_shapes=[pltpu.VMEM((2, tokens * heads + PAD, size), jnp.float32)],
        compiler_params=pltpu.CompilerParams(vmem_limit_bytes=VMEM_LIMIT),
        cost_estimate=pl.CostEstimate(flops=0, bytes_accessed=12 * tokens * heads * size * 2, transcendentals=0),
    )(*terms)


def scores_of(q, key, bias_ref, s):
    x = product_nt(q, key)
    blocks = bias_ref.shape[1]
    width = x.shape[0] // blocks
    return jnp.concatenate([x[a * width : (a + 1) * width] + bias_ref[s, a : a + 1] for a in range(blocks)], axis=0)


def twice(array):
    return jnp.concatenate([array, array], axis=1)


def fill_values(kv_refs, v_ref):
    for n, ref in enumerate(kv_refs):
        value = ref[0, 1]
        v_ref[n] = jnp.concatenate([value, jnp.ones_like(value)], axis=1)


def local_kernel(softmax_scale, bias_ref, q_ref, *refs):
    sources = len(LOCAL)
    kv_refs = refs[:sources]
    e_ref, o_ref, stat_ref, x_ref, v_ref = refs[sources:]
    scale2 = softmax_scale * LOG2E
    head_group, tokens, size = q_ref.shape
    state = {}
    fill_values(kv_refs, v_ref)

    def scores(g, n):
        x = scores_of(q_ref[g], kv_refs[n][0, 0], bias_ref, LOCAL[n])
        x_ref[g % 3, n] = x
        state["max", g] = jnp.maximum(state["max", g], x) if n else x

    def scores_end(g):
        state["top", g] = jnp.max(state.pop(("max", g)), axis=1, keepdims=True) * scale2

    def forward(g, n):
        e = jnp.exp2(x_ref[g % 3, n] * scale2 - state["top", g])
        narrow = e.astype(jnp.bfloat16)
        e_ref[g, n] = narrow
        part = product(narrow, v_ref[n])
        state["out", g] = state["out", g] + part if n else part

    def forward_end(g):
        out = state.pop(("out", g))
        o_ref[g] = out[:, :size]
        stat_ref[g, 0] = jnp.broadcast_to(state["top", g], (tokens, size))
        stat_ref[g, 1] = out[:, size:]

    every = range(sources)
    for g in range(2):
        for n in every:
            scores(g, n)
        scores_end(g)
    for g in range(head_group):
        for n in every:
            forward(g, n)
            if g + 2 < head_group:
                scores(g + 2, n)
        forward_end(g)
        if g + 2 < head_group:
            scores_end(g + 2)


def remote_kernel(softmax_scale, unused, bias_ref, q_ref, do_ref, part_ref, stat_ref, *refs):
    sources = len(REMOTE)
    kv_refs = refs[:sources]
    refs = refs[sources + unused :]
    o_ref, dq_ref, row_ref = refs[:3]
    term_refs = refs[3 : sources + 3]
    dk_ref, dv_ref, x_ref, e_ref, p_ref, d_ref, v_ref, k_ref = refs[sources + 3 :]
    scale2 = softmax_scale * LOG2E
    head_group, tokens, size = q_ref.shape
    state = {}
    fill_values(kv_refs, v_ref)
    for n in range(sources):
        k_ref[n * tokens : (n + 1) * tokens] = kv_refs[n][0, 0]

    def key(n):
        return kv_refs[n][0, 0]

    def scores(g, n):
        x = scores_of(q_ref[g], key(n), bias_ref, REMOTE[n])
        x_ref[g % 3, n] = x
        state["max", g] = jnp.maximum(state["max", g], x) if n else x

    def dprob(g, n):
        p_ref[g % 2, n] = product_nt(do_ref[g], kv_refs[n][0, 1])

    def scores_end(g):
        local, total = stat_ref[g, 0], stat_ref[g, 1]
        top = jnp.maximum(jnp.max(state.pop(("max", g)), axis=1, keepdims=True) * scale2, local)
        state["top", g] = top
        state["share", g] = jnp.exp2(local - top)
        state["part", g] = total * state["share", g]

    def forward(g, n):
        e = jnp.exp2(x_ref[g % 3, n] * scale2 - twice(state["top", g]))
        narrow = e.astype(jnp.bfloat16)
        e_ref[n, g * tokens : (g + 1) * tokens] = narrow
        part = product(narrow, v_ref[n])
        state["out", g] = state["out", g] + part if n else part

    def forward_end(g):
        q, do = q_ref[g], do_ref[g].astype(jnp.float32)
        out = state.pop(("out", g))
        share = state.pop(("share", g))
        inverse = 1.0 / (out[:, size:] + state.pop(("part", g)))
        attended = ((out[:, :size] + part_ref[g] * share) * inverse).astype(jnp.bfloat16)
        o_ref[g] = attended
        delta = jnp.sum(do * attended.astype(jnp.float32), axis=1, keepdims=True)
        state["delta", g] = delta
        row_ref[g, 0] = share * inverse
        row_ref[g, 1] = jnp.broadcast_to(delta, (tokens, size))
        state["scale", g] = inverse * softmax_scale
        dk_ref[:, g * tokens : (g + 1) * tokens] = (q.astype(jnp.float32) * state["scale", g]).astype(jnp.bfloat16).T
        dv_ref[:, g * tokens : (g + 1) * tokens] = (do * inverse).astype(jnp.bfloat16).T

    def backward(g, n):
        e = e_ref[n, g * tokens : (g + 1) * tokens]
        dscore = (e.astype(jnp.float32) * (p_ref[g % 2, n] - state["delta", g])).astype(jnp.bfloat16)
        state["d", g, n] = dscore
        d_ref[n, g * tokens : (g + 1) * tokens] = dscore

    def backward_end(g):
        dscore = jnp.concatenate([state.pop(("d", g, n)) for n in every], axis=1)
        dq_ref[g] = product(dscore, k_ref[...]) * state["scale", g]

    every = range(sources)
    for g in range(2):
        for n in every:
            scores(g, n)
        scores_end(g)
    for g in range(head_group):
        for n in every:
            forward(g, n)
            if g + 2 < head_group:
                scores(g + 2, n)
            dprob(g, n)
        forward_end(g)
        if g + 2 < head_group:
            scores_end(g + 2)
        if g:
            for n in every:
                backward(g - 1, n)
            backward_end(g - 1)
    for n in every:
        backward(head_group - 1, n)
    backward_end(head_group - 1)
    for n in every:
        term_refs[n][0, 0] = product(dk_ref[...], d_ref[n]).T.astype(jnp.bfloat16)
        term_refs[n][0, 1] = product(dv_ref[...], e_ref[n]).T.astype(jnp.bfloat16)


def rest_kernel(softmax_scale, unused, q_ref, do_ref, e_ref, part_ref, row_ref, *refs):
    sources = len(LOCAL)
    kv_refs = refs[:sources]
    refs = refs[sources + unused :]
    dq_ref = refs[0]
    term_refs = refs[1 : sources + 1]
    dk_ref, dv_ref, p_ref = refs[sources + 1 :]
    head_group = q_ref.shape[0]
    state = {}

    def dprob(g, n):
        p_ref[g % 2, n] = product_nt(do_ref[g], kv_refs[n][0, 1])

    def rows(g):
        share = row_ref[g, 0]
        state["delta", g] = twice(row_ref[g, 1])
        state["scale", g] = share * softmax_scale
        state["q", g] = (q_ref[g].astype(jnp.float32) * state["scale", g]).astype(jnp.bfloat16).T
        state["do", g] = (do_ref[g].astype(jnp.float32) * share).astype(jnp.bfloat16).T

    def backward(g, n):
        e = e_ref[g, n]
        dv = product(state["do", g], e)
        dscore = (e.astype(jnp.float32) * (p_ref[g % 2, n] - state["delta", g])).astype(jnp.bfloat16)
        part = product(dscore, kv_refs[n][0, 0])
        state["dq", g] = state["dq", g] + part if n else part
        dk = product(state["q", g], dscore)
        if g == 0:
            dk_ref[n] = dk
            dv_ref[n] = dv
        elif g < head_group - 1:
            dk_ref[n] += dk
            dv_ref[n] += dv
        else:
            term_refs[n][0, 0] = (dk_ref[n] + dk).T.astype(jnp.bfloat16)
            term_refs[n][0, 1] = (dv_ref[n] + dv).T.astype(jnp.bfloat16)

    every = range(sources)
    for n in every:
        dprob(0, n)
    rows(0)
    for g in range(head_group):
        if g + 1 < head_group:
            rows(g + 1)
        for n in every:
            backward(g, n)
            if g + 1 < head_group:
                dprob(g + 1, n)
        dq_ref[g] = (part_ref[g] + state.pop(("dq", g)) * state["scale", g]).astype(jnp.bfloat16)


def cost(products, heads, head_group, tokens, sources, size):
    scores = heads * head_group * tokens * tokens * sources
    return pl.CostEstimate(
        flops=2 * products * scores * size,
        bytes_accessed=8 * heads * head_group * tokens * size,
        transcendentals=scores,
    )


def attend(bias, queries, output_gradient, heads_all, head_group):
    tokens, size = queries.shape[1:]

    def rows(first):
        return pl.BlockSpec((head_group, tokens, size), lambda j: (first + j, 0, 0))

    def block(first, begin):
        return pl.BlockSpec((1, 2, tokens, size), lambda j: (first - begin + j, 0, 0, 0))

    def exps(first):
        return pl.BlockSpec((head_group, len(LOCAL), tokens, tokens), lambda j: (first + j, 0, 0, 0))

    def columns(first):
        return pl.BlockSpec((head_group, 2, tokens, size), lambda j: (first + j, 0, 0, 0))

    scale = size ** (-0.5)
    query_heads = heads_all * head_group
    wide = jax.ShapeDtypeStruct((query_heads, tokens, size), jnp.float32)
    double = jax.ShapeDtypeStruct((query_heads, 2, tokens, size), jnp.float32)
    narrow = jax.ShapeDtypeStruct((query_heads, tokens, size), jnp.bfloat16)
    params = pltpu.CompilerParams(vmem_limit_bytes=VMEM_LIMIT)

    def term(count):
        return jax.ShapeDtypeStruct((count, 2, tokens, size), jnp.bfloat16)

    def square(depth, count, kind=jnp.float32):
        return pltpu.VMEM((depth, count, tokens, tokens), kind)

    def local(own):
        n = len(LOCAL)
        return pl.pallas_call(
            functools.partial(local_kernel, scale),
            grid=(heads_all,),
            in_specs=[VMEM, rows(0)] + [block(0, 0)] * n,
            out_specs=[exps(0), rows(0), columns(0)],
            out_shape=[jax.ShapeDtypeStruct((query_heads, n, tokens, tokens), jnp.bfloat16), wide, double],
            scratch_shapes=[square(3, n), pltpu.VMEM((n, tokens, 2 * size), jnp.bfloat16)],
            compiler_params=params,
            cost_estimate=cost(2, heads_all, head_group, tokens, n, size),
        )(bias, in_hbm(queries), *own)

    def remote(heads, part, stat, others, chain):
        first, last = heads
        n = len(REMOTE)
        whole = [rows(first)] * 2 + [columns(first), block(first, 0)]
        return pl.pallas_call(
            functools.partial(remote_kernel, scale, len(chain)),
            grid=(last - first,),
            in_specs=[VMEM] + [rows(first)] * 3 + [columns(first)] + [block(first, begin) for _, begin in others] + [ANY] * len(chain),
            out_specs=whole + [block(0, 0)] * (n - 1),
            out_shape=[narrow, wide, double, term(heads_all)] + [term(last - first)] * (n - 1),
            scratch_shapes=[pltpu.VMEM((size, head_group * tokens), jnp.bfloat16)] * 2
            + [square(3, n), pltpu.VMEM((n, head_group * tokens, tokens), jnp.bfloat16), square(2, n), pltpu.VMEM((n, head_group * tokens, tokens), jnp.bfloat16), pltpu.VMEM((n, tokens, 2 * size), jnp.bfloat16), pltpu.VMEM((n * tokens, size), jnp.bfloat16)],
            input_output_aliases={5 + n + i: i for i in range(len(chain))},
            compiler_params=params,
            cost_estimate=cost(6, last - first, head_group, tokens, n, size),
        )(bias, in_hbm(queries), in_hbm(output_gradient), part, stat, *[a for a, _ in others], *chain)

    def rest(heads, e, part, row, own, chain):
        first, last = heads
        n = len(LOCAL)
        return pl.pallas_call(
            functools.partial(rest_kernel, scale, len(chain)),
            grid=(last - first,),
            in_specs=[rows(first)] * 2
            + [exps(first)]
            + [rows(first), columns(first)]
            + [block(first, 0)] * n
            + [ANY] * len(chain),
            out_specs=[rows(first)] + [block(0, 0)] * n,
            out_shape=[narrow] + [term(last - first)] * n,
            scratch_shapes=[pltpu.VMEM((n, size, tokens), jnp.float32)] * 2 + [square(2, n)],
            input_output_aliases={5 + n + i: i for i in range(len(chain))},
            compiler_params=params,
            cost_estimate=cost(4, last - first, head_group, tokens, n, size),
        )(in_hbm(queries), in_hbm(output_gradient), e, part, row, *own, *chain)

    return local, remote, rest


def shards(block_mask, queries, keys, values, output_gradient):
    count = lax.axis_size("seq")
    me = lax.axis_index("seq").astype(jnp.int32).reshape(1)
    tokens, kv_heads, size = keys.shape
    head_group = queries.shape[1] // kv_heads
    bits = partner_bits(count)
    q = jnp.transpose(queries, (1, 0, 2))
    dout = jnp.transpose(output_gradient, (1, 0, 2))
    whole = (0, kv_heads)
    groups = (whole,) + HALVES
    packed = dict(zip(groups, pack(keys, values, groups)))
    bias = mask_rows(me, block_mask, tokens, bits)
    far = {(HALVES[0], bit): from_partner(packed[HALVES[0]], "seq", bit) for bit in reversed(bits[2:])}
    core = from_partner(packed[whole], "seq", bits[0])
    near = {HALVES[0]: from_partner(packed[HALVES[0]], "seq", bits[1])}
    local, remote, rest = attend(bias, q, dout, kv_heads, head_group)
    own = [packed[whole], core]
    e, part, stat = local(own)
    for heads in HALVES[1:]:
        later = lax.optimization_barrier((packed[heads], stat))[0]
        far.update({(heads, bit): from_partner(later, "seq", bit) for bit in reversed(bits[2:])})
        near[heads] = from_partner(later, "seq", bits[1])
    chain, sent, terms, term_groups = [], [], [], []
    for heads in HALVES:
        others = [(near[heads], heads[0])] + [(far[heads, bit], heads[0]) for bit in bits[2:]]
        results = remote(heads, part, stat, others, chain)
        chain = results[:4]
        back = results[4:]
        for bit, term in reversed(list(zip(bits[2:], back))):
            sent.append(from_partner(term, "seq", bit))
            term_groups.append(heads)
    terms = list(sent)
    attended, grad_part, row, near_term = chain
    terms.append(from_partner(near_term, "seq", bits[1]))
    early = len(bits[2:]) * (len(HALVES) - 1)
    row = lax.optimization_barrier((row, *terms[:early]))[0]
    last_groups, last, chain = [whole], [], []
    for heads in HALVES:
        grad_queries, own_term, core_term = rest(heads, e, grad_part, row, own, chain)
        chain = [grad_queries]
        last += [from_partner(core_term, "seq", bits[0]), own_term]
        last_groups += [heads] * 2
    term_groups.append(whole)
    gathered = gather_terms(term_groups, terms, kv_heads)
    grad_keys, grad_values = sum_terms(last_groups, [gathered] + last, tokens, kv_heads, size)
    return (jnp.transpose(attended, (1, 0, 2)), jnp.transpose(grad_queries, (1, 0, 2)), grad_keys, grad_values)


def solution(mesh):
    rows = P(("groups", "seq"), None)
    cube = P(("groups", "seq"), None, None)
    return jax.shard_map(
        shards,
        mesh=mesh,
        in_specs=(rows, cube, cube, cube, cube),
        out_specs=(cube, cube, cube, cube),
        check_vma=False,
    )
```

```python
import functools

import jax
import jax.numpy as jnp
from jax import lax
from jax.experimental import pallas as pl
from jax.experimental.pallas import tpu as pltpu
from jax.sharding import PartitionSpec as P

LOG2E = 1.4426950408889634
MASKED = -1e30
VMEM_LIMIT = 24 * 2**20
PAD = 32
LOCAL = (0, 1)
REMOTE = (2, 3, 4)
HALVES = ((0, 2), (2, 4))


def from_partner(value, axis, apart):
    mask = 2**apart
    pairs = [(source, source ^ mask) for source in range(lax.axis_size(axis))]
    return lax.ppermute(value, axis, pairs)


def partner_bits(count):
    level = count.bit_length() - 1
    return (0, 1, level - 2, level - 1)


def product(left, right):
    return lax.dot_general(left, right, (((1,), (0,)), ((), ())), preferred_element_type=jnp.float32)


def product_nt(left, right):
    return lax.dot_general(left, right, (((1,), (1,)), ((), ())), preferred_element_type=jnp.float32)


VMEM = pl.BlockSpec(memory_space=pltpu.VMEM)
SMEM = pl.BlockSpec(memory_space=pltpu.SMEM)
ANY = pl.BlockSpec(memory_space=pl.ANY)


def in_hbm(array):
    return pltpu.with_memory_space_constraint(array, pltpu.HBM)


def pack_kernel(groups, k_ref, v_ref, *refs):
    outs, wide_ref = refs[:-1], refs[-1]
    tokens, heads, size = k_ref.shape
    for i, ref in enumerate((k_ref, v_ref)):
        wide_ref[i, : tokens * heads] = ref[...].astype(jnp.float32).reshape(tokens * heads, size)
        for h in range(heads):
            rows = wide_ref[i, pl.ds(h, tokens, stride=heads), :].astype(jnp.bfloat16)
            for (low, high), out in zip(groups, outs):
                if low <= h < high:
                    out[h - low, i] = rows


def pack(keys, values, groups):
    tokens, heads, size = keys.shape
    return pl.pallas_call(
        functools.partial(pack_kernel, groups),
        in_specs=[VMEM] * 2,
        out_specs=[VMEM] * len(groups),
        out_shape=[jax.ShapeDtypeStruct((high - low, 2, tokens, size), keys.dtype) for low, high in groups],
        scratch_shapes=[pltpu.VMEM((2, tokens * heads + PAD, size), jnp.float32)],
        compiler_params=pltpu.CompilerParams(vmem_limit_bytes=VMEM_LIMIT),
        cost_estimate=pl.CostEstimate(flops=0, bytes_accessed=6 * keys.size * 2, transcendentals=0),
    )(in_hbm(keys), in_hbm(values))


def mask_kernel(bits, me_ref, mask_ref, bias_ref):
    me = me_ref[0]
    blocks, columns = mask_ref.shape
    width = bias_ref.shape[2] // blocks
    mask = mask_ref[...]
    column = lax.broadcasted_iota(jnp.int32, (blocks, columns), 1)
    for s, device in enumerate([me] + [jnp.bitwise_xor(me, 1 << bit) for bit in bits]):
        for b in range(blocks):
            ones = jnp.sum(jnp.where(column == device * blocks + b, mask, 0), axis=1, keepdims=True)
            bias_ref[s, :, b * width : (b + 1) * width] = jnp.broadcast_to(
                jnp.where(ones > 0, 0.0, MASKED), (blocks, width)
            )


def mask_rows(me, block_mask, tokens, bits):
    return pl.pallas_call(
        functools.partial(mask_kernel, bits),
        in_specs=[SMEM, VMEM],
        out_specs=VMEM,
        out_shape=jax.ShapeDtypeStruct((len(bits) + 1, block_mask.shape[0], tokens), jnp.float32),
        compiler_params=pltpu.CompilerParams(vmem_limit_bytes=VMEM_LIMIT),
        cost_estimate=pl.CostEstimate(flops=0, bytes_accessed=2**14, transcendentals=0),
    )(me, in_hbm(block_mask))


def gather_kernel(groups, *refs):
    terms, out = refs[:-1], refs[-1]
    for h in range(out.shape[0]):
        parts = [t[h - g[0]].astype(jnp.float32) for g, t in zip(groups, terms) if g[0] <= h < g[1]]
        out[h] = functools.reduce(jnp.add, parts)


def gather_terms(groups, terms, heads):
    return pl.pallas_call(
        functools.partial(gather_kernel, groups),
        in_specs=[VMEM] * len(groups),
        out_specs=VMEM,
        out_shape=jax.ShapeDtypeStruct((heads,) + terms[0].shape[1:], jnp.float32),
        compiler_params=pltpu.CompilerParams(vmem_limit_bytes=VMEM_LIMIT),
        cost_estimate=pl.CostEstimate(flops=0, bytes_accessed=8 * 2**20, transcendentals=0),
    )(*terms)


def sum_kernel(groups, *refs):
    terms, (dk_ref, dv_ref, wide_ref) = refs[: len(groups)], refs[len(groups) :]
    tokens, heads, size = dk_ref.shape
    for i, ref in enumerate((dk_ref, dv_ref)):
        for h in range(heads):
            parts = [t[h - g[0], i].astype(jnp.float32) for g, t in zip(groups, terms) if g[0] <= h < g[1]]
            wide_ref[i, pl.ds(h, tokens, stride=heads), :] = functools.reduce(jnp.add, parts)
        ref[...] = wide_ref[i, : tokens * heads].astype(ref.dtype).reshape(tokens, heads, size)


def sum_terms(groups, terms, tokens, heads, size):
    out = jax.ShapeDtypeStruct((tokens, heads, size), jnp.bfloat16)
    return pl.pallas_call(
        functools.partial(sum_kernel, groups),
        in_specs=[VMEM] * len(groups),
        out_specs=[VMEM] * 2,
        out_shape=[out, out],
        scratch_shapes=[pltpu.VMEM((2, tokens * heads + PAD, size), jnp.float32)],
        compiler_params=pltpu.CompilerParams(vmem_limit_bytes=VMEM_LIMIT),
        cost_estimate=pl.CostEstimate(flops=0, bytes_accessed=12 * tokens * heads * size * 2, transcendentals=0),
    )(*terms)


def scores_of(q, key, bias_ref, s):
    x = product_nt(q, key)
    blocks = bias_ref.shape[1]
    width = x.shape[0] // blocks
    return jnp.concatenate([x[a * width : (a + 1) * width] + bias_ref[s, a : a + 1] for a in range(blocks)], axis=0)


def twice(array):
    return jnp.concatenate([array, array], axis=1)


def fill_values(kv_refs, v_ref):
    for n, ref in enumerate(kv_refs):
        value = ref[0, 1]
        v_ref[n] = jnp.concatenate([value, jnp.ones_like(value)], axis=1)


def local_kernel(softmax_scale, bias_ref, q_ref, *refs):
    sources = len(LOCAL)
    kv_refs = refs[:sources]
    e_ref, o_ref, stat_ref, x_ref, v_ref = refs[sources:]
    scale2 = softmax_scale * LOG2E
    head_group, tokens, size = q_ref.shape
    state = {}
    fill_values(kv_refs, v_ref)

    def scores(g, n):
        x = scores_of(q_ref[g], kv_refs[n][0, 0], bias_ref, LOCAL[n])
        x_ref[g % 3, n] = x
        state["max", g] = jnp.maximum(state["max", g], x) if n else x

    def scores_end(g):
        state["top", g] = jnp.max(state.pop(("max", g)), axis=1, keepdims=True) * scale2

    def forward(g, n):
        e = jnp.exp2(x_ref[g % 3, n] * scale2 - state["top", g])
        narrow = e.astype(jnp.bfloat16)
        e_ref[g, n] = narrow
        part = product(narrow, v_ref[n])
        state["out", g] = state["out", g] + part if n else part

    def forward_end(g):
        out = state.pop(("out", g))
        o_ref[g] = out[:, :size]
        stat_ref[g, 0] = jnp.broadcast_to(state["top", g], (tokens, size))
        stat_ref[g, 1] = out[:, size:]

    every = range(sources)
    for g in range(2):
        for n in every:
            scores(g, n)
        scores_end(g)
    for g in range(head_group):
        for n in every:
            forward(g, n)
            if g + 2 < head_group:
                scores(g + 2, n)
        forward_end(g)
        if g + 2 < head_group:
            scores_end(g + 2)


def remote_kernel(softmax_scale, unused, bias_ref, q_ref, do_ref, part_ref, stat_ref, *refs):
    sources = len(REMOTE)
    kv_refs = refs[:sources]
    refs = refs[sources + unused :]
    o_ref, dq_ref, row_ref = refs[:3]
    term_refs = refs[3 : sources + 3]
    dk_ref, dv_ref, x_ref, e_ref, p_ref, d_ref, v_ref, k_ref = refs[sources + 3 :]
    scale2 = softmax_scale * LOG2E
    head_group, tokens, size = q_ref.shape
    state = {}
    fill_values(kv_refs, v_ref)
    for n in range(sources):
        k_ref[n * tokens : (n + 1) * tokens] = kv_refs[n][0, 0]

    def key(n):
        return kv_refs[n][0, 0]

    def scores(g, n):
        x = scores_of(q_ref[g], key(n), bias_ref, REMOTE[n])
        x_ref[g % 3, n] = x
        state["max", g] = jnp.maximum(state["max", g], x) if n else x

    def dprob(g, n):
        p_ref[g % 2, n] = product_nt(do_ref[g], kv_refs[n][0, 1])

    def scores_end(g):
        local, total = stat_ref[g, 0], stat_ref[g, 1]
        top = jnp.maximum(jnp.max(state.pop(("max", g)), axis=1, keepdims=True) * scale2, local)
        state["top", g] = top
        state["share", g] = jnp.exp2(local - top)
        state["part", g] = total * state["share", g]

    def forward(g, n):
        e = jnp.exp2(x_ref[g % 3, n] * scale2 - twice(state["top", g]))
        narrow = e.astype(jnp.bfloat16)
        e_ref[n, g * tokens : (g + 1) * tokens] = narrow
        state["e", g, n] = narrow

    def forward_end(g):
        q, do = q_ref[g], do_ref[g].astype(jnp.float32)
        narrow = jnp.concatenate([state.pop(("e", g, n)) for n in every], axis=1)
        out = product(narrow, v_ref[...].reshape(sources * tokens, 2 * size))
        share = state.pop(("share", g))
        inverse = 1.0 / (out[:, size:] + state.pop(("part", g)))
        attended = ((out[:, :size] + part_ref[g] * share) * inverse).astype(jnp.bfloat16)
        o_ref[g] = attended
        delta = jnp.sum(do * attended.astype(jnp.float32), axis=1, keepdims=True)
        state["delta", g] = delta
        row_ref[g, 0] = share * inverse
        row_ref[g, 1] = jnp.broadcast_to(delta, (tokens, size))
        state["scale", g] = inverse * softmax_scale
        dk_ref[:, g * tokens : (g + 1) * tokens] = (q.astype(jnp.float32) * state["scale", g]).astype(jnp.bfloat16).T
        dv_ref[:, g * tokens : (g + 1) * tokens] = (do * inverse).astype(jnp.bfloat16).T

    def backward(g, n):
        e = e_ref[n, g * tokens : (g + 1) * tokens]
        dscore = (e.astype(jnp.float32) * (p_ref[g % 2, n] - state["delta", g])).astype(jnp.bfloat16)
        state["d", g, n] = dscore
        d_ref[n, g * tokens : (g + 1) * tokens] = dscore

    def backward_end(g):
        dscore = jnp.concatenate([state.pop(("d", g, n)) for n in every], axis=1)
        dq_ref[g] = product(dscore, k_ref[...]) * state["scale", g]

    every = range(sources)
    for g in range(2):
        for n in every:
            scores(g, n)
        scores_end(g)
    for g in range(head_group):
        for n in every:
            forward(g, n)
            if g + 2 < head_group:
                scores(g + 2, n)
            dprob(g, n)
        forward_end(g)
        if g + 2 < head_group:
            scores_end(g + 2)
        if g:
            for n in every:
                backward(g - 1, n)
            backward_end(g - 1)
    for n in every:
        backward(head_group - 1, n)
    backward_end(head_group - 1)
    for n in every:
        term_refs[n][0, 0] = product(dk_ref[...], d_ref[n]).T.astype(jnp.bfloat16)
        term_refs[n][0, 1] = product(dv_ref[...], e_ref[n]).T.astype(jnp.bfloat16)


def rest_kernel(softmax_scale, unused, q_ref, do_ref, e_ref, part_ref, row_ref, *refs):
    sources = len(LOCAL)
    kv_refs = refs[:sources]
    refs = refs[sources + unused :]
    dq_ref = refs[0]
    term_refs = refs[1 : sources + 1]
    dk_ref, dv_ref, p_ref = refs[sources + 1 :]
    head_group = q_ref.shape[0]
    state = {}

    def dprob(g, n):
        p_ref[g % 2, n] = product_nt(do_ref[g], kv_refs[n][0, 1])

    def rows(g):
        share = row_ref[g, 0]
        state["delta", g] = twice(row_ref[g, 1])
        state["scale", g] = share * softmax_scale
        state["q", g] = (q_ref[g].astype(jnp.float32) * state["scale", g]).astype(jnp.bfloat16).T
        state["do", g] = (do_ref[g].astype(jnp.float32) * share).astype(jnp.bfloat16).T

    def backward(g, n):
        e = e_ref[g, n]
        dv = product(state["do", g], e)
        dscore = (e.astype(jnp.float32) * (p_ref[g % 2, n] - state["delta", g])).astype(jnp.bfloat16)
        part = product(dscore, kv_refs[n][0, 0])
        state["dq", g] = state["dq", g] + part if n else part
        dk = product(state["q", g], dscore)
        if g == 0:
            dk_ref[n] = dk
            dv_ref[n] = dv
        elif g < head_group - 1:
            dk_ref[n] += dk
            dv_ref[n] += dv
        else:
            term_refs[n][0, 0] = (dk_ref[n] + dk).T.astype(jnp.bfloat16)
            term_refs[n][0, 1] = (dv_ref[n] + dv).T.astype(jnp.bfloat16)

    every = range(sources)
    for n in every:
        dprob(0, n)
    rows(0)
    for g in range(head_group):
        if g + 1 < head_group:
            rows(g + 1)
        for n in every:
            backward(g, n)
            if g + 1 < head_group:
                dprob(g + 1, n)
        dq_ref[g] = (part_ref[g] + state.pop(("dq", g)) * state["scale", g]).astype(jnp.bfloat16)


def cost(products, heads, head_group, tokens, sources, size):
    scores = heads * head_group * tokens * tokens * sources
    return pl.CostEstimate(
        flops=2 * products * scores * size,
        bytes_accessed=8 * heads * head_group * tokens * size,
        transcendentals=scores,
    )


def attend(bias, queries, output_gradient, heads_all, head_group):
    tokens, size = queries.shape[1:]

    def rows(first):
        return pl.BlockSpec((head_group, tokens, size), lambda j: (first + j, 0, 0))

    def block(first, begin):
        return pl.BlockSpec((1, 2, tokens, size), lambda j: (first - begin + j, 0, 0, 0))

    def exps(first):
        return pl.BlockSpec((head_group, len(LOCAL), tokens, tokens), lambda j: (first + j, 0, 0, 0))

    def columns(first):
        return pl.BlockSpec((head_group, 2, tokens, size), lambda j: (first + j, 0, 0, 0))

    scale = size ** (-0.5)
    query_heads = heads_all * head_group
    wide = jax.ShapeDtypeStruct((query_heads, tokens, size), jnp.float32)
    double = jax.ShapeDtypeStruct((query_heads, 2, tokens, size), jnp.float32)
    narrow = jax.ShapeDtypeStruct((query_heads, tokens, size), jnp.bfloat16)
    params = pltpu.CompilerParams(vmem_limit_bytes=VMEM_LIMIT)

    def term(count):
        return jax.ShapeDtypeStruct((count, 2, tokens, size), jnp.bfloat16)

    def square(depth, count, kind=jnp.float32):
        return pltpu.VMEM((depth, count, tokens, tokens), kind)

    def local(own):
        n = len(LOCAL)
        return pl.pallas_call(
            functools.partial(local_kernel, scale),
            grid=(heads_all,),
            in_specs=[VMEM, rows(0)] + [block(0, 0)] * n,
            out_specs=[exps(0), rows(0), columns(0)],
            out_shape=[jax.ShapeDtypeStruct((query_heads, n, tokens, tokens), jnp.bfloat16), wide, double],
            scratch_shapes=[square(3, n), pltpu.VMEM((n, tokens, 2 * size), jnp.bfloat16)],
            compiler_params=params,
            cost_estimate=cost(2, heads_all, head_group, tokens, n, size),
        )(bias, in_hbm(queries), *own)

    def remote(heads, part, stat, others, chain):
        first, last = heads
        n = len(REMOTE)
        whole = [rows(first)] * 2 + [columns(first), block(first, 0)]
        return pl.pallas_call(
            functools.partial(remote_kernel, scale, len(chain)),
            grid=(last - first,),
            in_specs=[VMEM] + [rows(first)] * 3 + [columns(first)] + [block(first, begin) for _, begin in others] + [ANY] * len(chain),
            out_specs=whole + [block(0, 0)] * (n - 1),
            out_shape=[narrow, wide, double, term(heads_all)] + [term(last - first)] * (n - 1),
            scratch_shapes=[pltpu.VMEM((size, head_group * tokens), jnp.bfloat16)] * 2
            + [square(3, n), pltpu.VMEM((n, head_group * tokens, tokens), jnp.bfloat16), square(2, n), pltpu.VMEM((n, head_group * tokens, tokens), jnp.bfloat16), pltpu.VMEM((n, tokens, 2 * size), jnp.bfloat16), pltpu.VMEM((n * tokens, size), jnp.bfloat16)],
            input_output_aliases={5 + n + i: i for i in range(len(chain))},
            compiler_params=params,
            cost_estimate=cost(6, last - first, head_group, tokens, n, size),
        )(bias, in_hbm(queries), in_hbm(output_gradient), part, stat, *[a for a, _ in others], *chain)

    def rest(heads, e, part, row, own, chain):
        first, last = heads
        n = len(LOCAL)
        return pl.pallas_call(
            functools.partial(rest_kernel, scale, len(chain)),
            grid=(last - first,),
            in_specs=[rows(first)] * 2
            + [exps(first)]
            + [rows(first), columns(first)]
            + [block(first, 0)] * n
            + [ANY] * len(chain),
            out_specs=[rows(first)] + [block(0, 0)] * n,
            out_shape=[narrow] + [term(last - first)] * n,
            scratch_shapes=[pltpu.VMEM((n, size, tokens), jnp.float32)] * 2 + [square(2, n)],
            input_output_aliases={5 + n + i: i for i in range(len(chain))},
            compiler_params=params,
            cost_estimate=cost(4, last - first, head_group, tokens, n, size),
        )(in_hbm(queries), in_hbm(output_gradient), e, part, row, *own, *chain)

    return local, remote, rest


def shards(block_mask, queries, keys, values, output_gradient):
    count = lax.axis_size("seq")
    me = lax.axis_index("seq").astype(jnp.int32).reshape(1)
    tokens, kv_heads, size = keys.shape
    head_group = queries.shape[1] // kv_heads
    bits = partner_bits(count)
    q = jnp.transpose(queries, (1, 0, 2))
    dout = jnp.transpose(output_gradient, (1, 0, 2))
    whole = (0, kv_heads)
    groups = (whole,) + HALVES
    packed = dict(zip(groups, pack(keys, values, groups)))
    bias = mask_rows(me, block_mask, tokens, bits)
    far = {(HALVES[0], bit): from_partner(packed[HALVES[0]], "seq", bit) for bit in reversed(bits[2:])}
    core = from_partner(packed[whole], "seq", bits[0])
    near = {HALVES[0]: from_partner(packed[HALVES[0]], "seq", bits[1])}
    local, remote, rest = attend(bias, q, dout, kv_heads, head_group)
    own = [packed[whole], core]
    e, part, stat = local(own)
    for heads in HALVES[1:]:
        later = lax.optimization_barrier((packed[heads], stat))[0]
        far.update({(heads, bit): from_partner(later, "seq", bit) for bit in reversed(bits[2:])})
        near[heads] = from_partner(later, "seq", bits[1])
    chain, sent, terms, term_groups = [], [], [], []
    for heads in HALVES:
        others = [(near[heads], heads[0])] + [(far[heads, bit], heads[0]) for bit in bits[2:]]
        results = remote(heads, part, stat, others, chain)
        chain = results[:4]
        back = results[4:]
        for bit, term in reversed(list(zip(bits[2:], back))):
            sent.append(from_partner(term, "seq", bit))
            term_groups.append(heads)
    terms = list(sent)
    attended, grad_part, row, near_term = chain
    terms.append(from_partner(near_term, "seq", bits[1]))
    early = len(bits[2:]) * (len(HALVES) - 1)
    row = lax.optimization_barrier((row, *terms[:early]))[0]
    last_groups, last, chain = [whole], [], []
    for heads in HALVES:
        grad_queries, own_term, core_term = rest(heads, e, grad_part, row, own, chain)
        chain = [grad_queries]
        last += [from_partner(core_term, "seq", bits[0]), own_term]
        last_groups += [heads] * 2
    term_groups.append(whole)
    gathered = gather_terms(term_groups, terms, kv_heads)
    grad_keys, grad_values = sum_terms(last_groups, [gathered] + last, tokens, kv_heads, size)
    return (jnp.transpose(attended, (1, 0, 2)), jnp.transpose(grad_queries, (1, 0, 2)), grad_keys, grad_values)


def solution(mesh):
    rows = P(("groups", "seq"), None)
    cube = P(("groups", "seq"), None, None)
    return jax.shard_map(
        shards,
        mesh=mesh,
        in_specs=(rows, cube, cube, cube, cube),
        out_specs=(cube, cube, cube, cube),
        check_vma=False,
    )
```
